256 devices in a mesh: rows: 32 (over x, z), cols: 8 (over y, core).
Axes of the slice: x: 4, y: 4, z: 8, core: 2. Of those that a mesh axis runs over, the one named last changes fastest.
Arguments:
- features: bfloat16 [128, 131072], P('cols', 'rows'), may hold values from -6 to 6
- node_order: int32 [131072], P('rows'), may hold values from 0 to 131071, as said below
- tile_row: int32 [4096], P('rows'), may hold values from 0 to 1023, as said below
- tile_col: int32 [4096], P('rows'), may hold values from 0 to 1023, as said below
- tile_vals: bfloat16 [4096, 128, 128], P('rows'), may hold values from 0 to 0.099609375
- weight: bfloat16 [128, 128], replicated, may hold values from -0.5 to 0.5
- grad_out: bfloat16 [128, 131072], P('cols', 'rows'), may hold values from -6 to 6
Outputs:
- activated: bfloat16 [128, 131072], P('cols', 'rows')
- feat_grads: bfloat16 [128, 131072], P('cols', 'rows')
- weight_grad: float32 [128, 128], P(None, 'cols')
The draws below stay inside these ranges and needn't reach their ends.
Inputs may be any that keep to these rules, and one draw needn't show every extreme that they name: Within each aligned run of 4096 entries, node_order is a permutation of the node numbers of that run. Tile t lies in the row blocks of its own index of rows: tile_row[t] // 32 == t // 128. Among the 128 tiles of one index of rows, the column blocks that belong to any one other index (tile_col // 32) are at most 8 distinct ones; every index of rows reaches 8 for some other index. Every row block has a tile on its own diagonal.
All inputs are finite; a program needn't handle non-finite values.
Results may differ from the reference program's by a relative error of at most 0.014.
Values may be sent and summed in bfloat16 or wider, within the bound.
No kernel may reach another device: no remote copies, remote signals or barrier semaphores. Data moves between devices by JAX's collectives and lax.ppermute only.
A program may use at most 128 MiB of HBM per device.

```python
import jax
import jax.numpy as jnp
from jax import lax

F = 128
TB = 128
TPB = 4
NB_DEV = 32
SLOTS = 8
TILES_DEV = 128
NODES = 131072
NTILES = 4096
N_ROWS = 32


def tile_pattern(key):
    key = jax.random.fold_in(key, 11)
    key_rank, key_first, key_second, key_coin, key_slot, key_local, key_row = jax.random.split(key, 7)
    tile_total = TILES_DEV * N_ROWS
    positions = jnp.arange(tile_total, dtype=jnp.int32)
    device_ids = positions // TILES_DEV
    within = positions % TILES_DEV
    tile_kind = within % TPB
    series = within // TPB
    row_local = jnp.where(tile_kind == 0, series, jax.random.randint(key_row, (tile_total,), 0, NB_DEV))
    row_ids = device_ids * NB_DEV + row_local
    scores = jax.random.randint(key_rank, (N_ROWS, N_ROWS, NB_DEV), 0, 1 << 20) * NB_DEV + jnp.arange(NB_DEV, dtype=jnp.int32)
    allowed = jnp.argsort(scores, axis=-1, stable=True)[..., :SLOTS]
    first_pick = jax.random.randint(key_first, (tile_total,), 0, N_ROWS)
    second_pick = jax.random.randint(key_second, (tile_total,), 0, N_ROWS)
    hub_peer = first_pick * second_pick // N_ROWS
    coin_flip = jax.random.randint(key_coin, (tile_total,), 0, 2)
    peer_ids = jnp.where(coin_flip == 0, device_ids, hub_peer)
    forced = (tile_kind == 1) & (series < SLOTS)
    peer_ids = jnp.where(forced, (device_ids + 1) % N_ROWS, peer_ids)
    slot_ids = jax.random.randint(key_slot, (tile_total,), 0, SLOTS)
    slot_ids = jnp.where(forced, series, slot_ids)
    remote_block = allowed[device_ids, peer_ids, slot_ids]
    local_block = jax.random.randint(key_local, (tile_total,), 0, NB_DEV)
    col_block = jnp.where(peer_ids == device_ids, local_block, remote_block)
    col_ids = peer_ids * NB_DEV + col_block
    col_ids = jnp.where(tile_kind == 0, row_ids, col_ids)
    return (row_ids.astype(jnp.int32), col_ids.astype(jnp.int32))


def draw_tile_row(key, part):
    return tile_pattern(key)[0]


def draw_tile_col(key, part):
    return tile_pattern(key)[1]


def draw_node_order(key, part):
    key = jax.random.fold_in(key, 5)
    device_keys = jax.random.split(key, N_ROWS)
    shuffles = jax.vmap(lambda one_key: jax.random.permutation(one_key, NB_DEV * TB))(device_keys)
    offsets = jnp.arange(N_ROWS, dtype=jnp.int32)[:, None] * (NB_DEV * TB)
    return (shuffles + offsets).reshape(-1).astype(jnp.int32)


def block_levels(key, dims, cuts, smallest, top_value):
    factor_of = 1.0
    for axis_at, parts in cuts:
        draws = jax.random.uniform(jax.random.fold_in(jax.random.fold_in(key, 6), axis_at), (parts,), jnp.float32, smallest / len(cuts), top_value / len(cuts))
        factor_of = factor_of * jnp.repeat(jnp.exp(draws), dims[axis_at] // parts).reshape((-1,) + (1,) * (len(dims) - 1 - axis_at))
    return factor_of


def gaussian(key, extent, scale, bound, cuts=(), held_as=jnp.bfloat16):
    factor_of = block_levels(key, extent, cuts, -0.22, 0.18) if cuts else 1.0
    result = jax.random.normal(key, extent, jnp.float32) * scale * factor_of
    return jnp.minimum(jnp.maximum(result, -bound), bound).astype(held_as)


def setup_inputs(seed: int = 0) -> dict:
    seeds = jax.random.split(jax.random.key(seed), 8)
    return {
        "features": gaussian(seeds[0], (F, NODES), 1.0, 6.0, ((0, 8), (1, 32))),
        "node_order": draw_node_order(jax.random.fold_in(seeds[7], 71), 0),
        "tile_row": draw_tile_row(jax.random.fold_in(seeds[7], 71), 0),
        "tile_col": draw_tile_col(jax.random.fold_in(seeds[7], 71), 0),
        "tile_vals": jnp.clip(0.099609375 * jax.random.uniform(seeds[4], (NTILES, TB, TB), jnp.float32) ** block_levels(seeds[4], (NTILES, TB, TB), ((0, 32),), -0.2, 0.2), 0.0, 0.099609375).astype(jnp.bfloat16),
        "weight": gaussian(seeds[5], (F, F), F ** -0.5, 0.5),
        "grad_out": gaussian(seeds[6], (F, NODES), 1.0, 6.0, ((0, 8), (1, 32))),
    }


def reference(features, node_order, tile_row, tile_col, tile_vals, weight, grad_out):
    node_count = NB_DEV * TB * N_ROWS
    block_count = NB_DEV * N_ROWS
    permuted = jnp.take(features, node_order, axis=1)
    feat_blocks = permuted.reshape(F, block_count, TB)
    group_rows = tile_row.reshape(N_ROWS, TILES_DEV)
    group_cols = tile_col.reshape(N_ROWS, TILES_DEV)
    group_vals = tile_vals.reshape(N_ROWS, TILES_DEV, TB, TB)
    row_bases = (jnp.arange(N_ROWS, dtype=jnp.int32) * NB_DEV).astype(jnp.int32)

    def forward_group(inputs):
        row_base, row_ids, col_ids, tile_block = inputs
        gathered = jnp.take(feat_blocks, col_ids, axis=1).astype(jnp.float32)
        products = jnp.einsum("ftm,tnm->tfn", gathered, tile_block.astype(jnp.float32))
        return jax.ops.segment_sum(products, (row_ids - row_base).astype(jnp.int32), num_segments=NB_DEV)

    summed = lax.map(forward_group, (row_bases, group_rows, group_cols, group_vals))
    aggregated = summed.reshape(block_count, F, TB).transpose(1, 0, 2).reshape(F, node_count).astype(jnp.bfloat16)
    pre_act = jnp.dot(weight.T, aggregated, preferred_element_type=jnp.float32)
    activated = jax.nn.silu(pre_act).astype(jnp.bfloat16)
    logistic = jax.nn.sigmoid(pre_act)
    pre_grad = (grad_out.astype(jnp.float32) * logistic * (1.0 + pre_act * (1.0 - logistic))).astype(jnp.bfloat16)
    weight_grad = jnp.dot(aggregated, pre_grad.T, preferred_element_type=jnp.float32) * (float(node_count) ** -0.5)
    agg_grad = jnp.dot(weight, pre_grad, preferred_element_type=jnp.float32).astype(jnp.bfloat16)
    grad_blocks = agg_grad.reshape(F, block_count, TB)

    def back_group(carry_sum, inputs):
        row_ids, col_ids, tile_block = inputs
        row_grads = jnp.take(grad_blocks, row_ids, axis=1).astype(jnp.float32)
        back_terms = jnp.einsum("ftn,tnm->tfm", row_grads, tile_block.astype(jnp.float32))
        return carry_sum.at[col_ids].add(back_terms), None

    start_sum = jnp.zeros((block_count, F, TB), jnp.float32)
    carry_sum, unused = lax.scan(back_group, start_sum, (group_rows, group_cols, group_vals))
    node_grads = carry_sum.transpose(1, 0, 2).reshape(F, node_count)
    feat_grads = jnp.zeros((F, node_count), jnp.float32).at[:, node_order].set(node_grads).astype(jnp.bfloat16)
    return activated, feat_grads, weight_grad
```

```python
import functools

import jax
import jax.numpy as jnp
from jax import lax
from jax.experimental import pallas as pl
from jax.experimental.pallas import tpu as pltpu
from jax.sharding import PartitionSpec as P

BF16 = jnp.bfloat16
F32 = jnp.float32
I32 = jnp.int32
SLOTS = 8
STEP = 16
VMEM = pl.BlockSpec(memory_space=pltpu.VMEM)
SMEM = pl.BlockSpec(memory_space=pltpu.SMEM)
NN = (((1,), (0,)), ((), ()))
NT = (((1,), (1,)), ((), ()))
TN = (((0,), (0,)), ((), ()))


def params(**kw):
    return pltpu.CompilerParams(vmem_limit_bytes=48 << 20, **kw)


def cost(flops, bytes_accessed):
    return pl.CostEstimate(flops=flops, bytes_accessed=bytes_accessed, transcendentals=0)


def dot(a, b, dims):
    return lax.dot_general(a, b, dims, preferred_element_type=F32)


def index_kernel(row_ref, col_ref, want_ref, place_ref, local_ref):
    peers = want_ref.shape[0]
    blocks = 32
    col = col_ref[...]
    row = row_ref[...]
    peer, block = col >> 5, col & 31
    tiles = col.shape[1]
    of_peer = (lax.broadcasted_iota(I32, (peers, tiles), 0) == peer).astype(F32)
    of_block = (lax.broadcasted_iota(I32, (blocks, tiles), 0) == block).astype(F32)
    counts = dot(of_peer.astype(BF16), of_block.astype(BF16), NT)
    present = (counts > 0.5).astype(F32)
    before = (
        lax.broadcasted_iota(I32, (blocks, blocks), 0)
        < lax.broadcasted_iota(I32, (blocks, blocks), 1)
    ).astype(F32)
    rank = dot(present.astype(BF16), before.astype(BF16), NN)
    number = lax.broadcasted_iota(I32, (peers, blocks), 1).astype(F32)
    lane = lax.broadcasted_iota(I32, (peers, 128), 1)
    want = jnp.zeros((peers, 128), F32)
    for s in range(SLOTS):
        chosen = jnp.sum(
            jnp.where(rank == float(s), present * number, 0.0), axis=1, keepdims=True
        )
        want = jnp.where(lane == s, chosen, want)
    want_ref[...] = want.astype(I32).reshape(peers, 1, 128)
    rank_of = dot(rank.astype(BF16), of_peer.astype(BF16), TN)
    tile_rank = jnp.sum(rank_of * of_block, axis=0, keepdims=True).astype(I32)
    own = peer == (row >> 5)
    place_ref[...] = jnp.where(own, peers * SLOTS + block, peer * SLOTS + tile_rank)
    local_ref[...] = row & 31


def permute_kernel(features_ref, order_ref, out_ref, blocked):
    count = order_ref.shape[0]
    width = features_ref.shape[0]
    for s in range(count):
        blocked[s * width : (s + 1) * width, :] = features_ref[:, s * 128 : (s + 1) * 128]
    low = lax.broadcasted_iota(I32, (128, 256), 0)
    for j in range(0, count, 2):
        o = jnp.concatenate([order_ref[j : j + 1, :], order_ref[j + 1 : j + 2, :]], axis=1)
        o = o & (count * 128 - 1)
        pick = jnp.where(low == (o & 127), 1.0, 0.0).astype(BF16)
        high = o >> 7
        spread = dot(blocked[...], pick, NN)
        total = jnp.zeros((width, 256), F32)
        for s in range(count):
            total = total + jnp.where(high == s, spread[s * width : (s + 1) * width], 0.0)
        total = total.astype(BF16)
        out_ref[j] = total[:, :128]
        out_ref[j + 1] = total[:, 128:]


def pack_kernel(asked_ref, blocks_ref, send_ref):
    for p in range(send_ref.shape[0]):
        for s in range(SLOTS):
            send_ref[p, s] = blocks_ref[asked_ref[p, 0, s]]


def forward_kernel(place_ref, local_ref, got_ref, own_ref, grad_ref, tiles_ref, out_ref, feats, prod, total):
    step = pl.program_id(0)
    slots = got_ref.shape[0] * SLOTS
    groups = out_ref.shape[0]
    per = out_ref.shape[1] // 2

    @pl.when(step == 0)
    def _():
        total[...] = jnp.zeros_like(total)
        for p in range(got_ref.shape[0]):
            feats[p * SLOTS : (p + 1) * SLOTS] = got_ref[p]
        feats[slots:] = own_ref[...]
        for c in range(groups):
            for b in range(per):
                at = (c * per + b) * 128
                out_ref[c, per + b] = grad_ref[:, at : at + 128]

    for t in range(STEP):
        prod[t] = dot(feats[place_ref[0, step * STEP + t]], tiles_ref[t], NT)
    for t in range(STEP):
        r = local_ref[0, step * STEP + t]
        total[r] = total[r] + prod[t]

    @pl.when(step == pl.num_programs(0) - 1)
    def _():
        for c in range(groups):
            for b in range(per):
                out_ref[c, b] = total[c * per + b].astype(BF16)


def dense_kernel(weight_ref, got_ref, out_ref):
    groups, _, width, _ = got_ref.shape
    per = got_ref.shape[1] // 2
    inputs = groups * width
    weight = weight_ref[...]
    weight_t = weight.astype(F32).T.astype(BF16)
    part = jnp.zeros((inputs, inputs), F32)
    for b in range(per):
        agg = got_ref[:, b].reshape(inputs, 128)
        grad = got_ref[:, per + b].reshape(inputs, 128).astype(F32)
        pre = dot(weight_t, agg, NN)
        logistic = jax.nn.sigmoid(pre)
        act = (pre * logistic).astype(BF16)
        pre_grad = (grad * logistic * (1.0 + pre * (1.0 - logistic))).astype(BF16)
        agg_grad = dot(weight, pre_grad, NN).astype(BF16)
        part = part + dot(pre_grad, agg, NT)
        out_ref[:, b] = agg_grad.reshape(groups, width, 128)
        out_ref[:, per + b] = act.reshape(groups, width, 128)
    high = part.astype(BF16)
    out_ref[:, 2 * per] = high.reshape(groups, width, 128)
    out_ref[:, 2 * per + 1] = (part - high.astype(F32)).astype(BF16).reshape(groups, width, 128)


def backward_kernel(place_ref, local_ref, got_ref, tiles_ref, send_ref, own_ref, act_ref, prod, total):
    step = pl.program_id(0)
    groups = got_ref.shape[0]
    per = (got_ref.shape[1] - 2) // 2
    peers = send_ref.shape[0]

    @pl.when(step == 0)
    def _():
        total[...] = jnp.zeros_like(total)
        part = got_ref[0, 2 * per].astype(F32) + got_ref[0, 2 * per + 1].astype(F32)
        for c in range(1, groups):
            part = part + got_ref[c, 2 * per].astype(F32) + got_ref[c, 2 * per + 1].astype(F32)
        part = part.astype(BF16)
        for p in range(peers):
            send_ref[p, SLOTS] = part
        for c in range(groups):
            for b in range(per):
                at = (c * per + b) * 128
                act_ref[:, at : at + 128] = got_ref[c, per + b]

    for t in range(STEP):
        r = local_ref[0, step * STEP + t]
        prod[t] = dot(got_ref[r // per, r % per], tiles_ref[t], NN)
    for t in range(STEP):
        d = place_ref[0, step * STEP + t]
        total[d] = total[d] + prod[t]

    @pl.when(step == pl.num_programs(0) - 1)
    def _():
        for p in range(peers):
            send_ref[p, :SLOTS] = total[p * SLOTS : (p + 1) * SLOTS].astype(BF16)
        own_ref[...] = total[peers * SLOTS :]


def final_kernel(scale, asked_ref, got_ref, own_ref, order_ref, grads_ref, weight_ref, total, spread, pick):
    peers = got_ref.shape[0]
    count = order_ref.shape[0]
    width = grads_ref.shape[0]
    total[...] = own_ref[...]
    part = got_ref[0, SLOTS].astype(F32)
    for p in range(1, peers):
        part = part + got_ref[p, SLOTS].astype(F32)
    weight_ref[...] = (part * scale).T
    for p in range(peers):
        for s in range(SLOTS):
            at = asked_ref[p, 0, s]
            total[at] = total[at] + got_ref[p, s].astype(F32)
    low = lax.broadcasted_iota(I32, (128, 128), 0)
    for j in range(count):
        o = order_ref[j : j + 1, :] & (count * 128 - 1)
        lanes = slice(j * 128, (j + 1) * 128)
        pick[:, lanes] = jnp.where(low == (o & 127), 1.0, 0.0).astype(BF16)
        high = o >> 7
        value = total[j]
        for s in range(count):
            spread[s * width : (s + 1) * width, lanes] = jnp.where(high == s, value, 0.0).astype(BF16)
    result = dot(spread[...], pick[...], NT).astype(BF16)
    for s in range(count):
        grads_ref[:, s * 128 : (s + 1) * 128] = result[s * width : (s + 1) * width, :]


def shards(features, node_order, tile_row, tile_col, tile_vals, weight, grad_out):
    width, span = features.shape
    tiles, size, _ = tile_vals.shape
    count = span // size
    peers = lax.axis_size("rows")
    groups = lax.axis_size("cols")
    per = count // groups
    order = node_order.reshape(count, size)
    steps = tiles // STEP

    with jax.named_scope("index"):
        want, place, local = pl.pallas_call(
            index_kernel,
            out_shape=(
                jax.ShapeDtypeStruct((peers, 1, 128), I32),
                jax.ShapeDtypeStruct((1, tiles), I32),
                jax.ShapeDtypeStruct((1, tiles), I32),
            ),
            in_specs=[VMEM, VMEM],
            out_specs=(VMEM, VMEM, VMEM),
            compiler_params=params(),
        )(tile_row.reshape(1, tiles), tile_col.reshape(1, tiles))
        asked = lax.all_to_all(want, "rows", 0, 0, tiled=True)

    with jax.named_scope("permute"):
        own = pl.pallas_call(
            permute_kernel,
            out_shape=jax.ShapeDtypeStruct((count, width, size), BF16),
            in_specs=[VMEM, VMEM],
            out_specs=VMEM,
            scratch_shapes=[pltpu.VMEM((count * width, size), BF16)],
            compiler_params=params(),
            cost_estimate=cost(2 * 512 * 128 * 4096, 1 << 20),
        )(features, order)

    with jax.named_scope("pack"):
        send = pl.pallas_call(
            pack_kernel,
            out_shape=jax.ShapeDtypeStruct((peers, SLOTS, width, size), BF16),
            in_specs=[SMEM, VMEM],
            out_specs=VMEM,
            compiler_params=params(),
        )(asked, own)
        got = lax.all_to_all(send, "rows", 0, 0, tiled=True)

    whole = lambda *shape: pl.BlockSpec(shape, lambda i: (0,) * len(shape))
    tile_spec = pl.BlockSpec((STEP, size, size), lambda i: (i, 0, 0))

    with jax.named_scope("forward"):
        mixed = pl.pallas_call(
            forward_kernel,
            out_shape=jax.ShapeDtypeStruct((groups, 2 * per, width, size), BF16),
            grid=(steps,),
            in_specs=[
                SMEM,
                SMEM,
                whole(peers, SLOTS, width, size),
                whole(count, width, size),
                whole(width, span),
                tile_spec,
            ],
            out_specs=whole(groups, 2 * per, width, size),
            scratch_shapes=[
                pltpu.VMEM((peers * SLOTS + count, width, size), BF16),
                pltpu.VMEM((STEP, width, size), F32),
                pltpu.VMEM((count, width, size), F32),
            ],
            compiler_params=params(dimension_semantics=("arbitrary",)),
            cost_estimate=cost(2 * tiles * width * size * size, 6 << 20),
        )(place, local, got, own, grad_out, tile_vals)
        mixed = lax.all_to_all(mixed, "cols", 0, 0, tiled=True)

    with jax.named_scope("dense"):
        back = pl.pallas_call(
            dense_kernel,
            out_shape=jax.ShapeDtypeStruct((groups, 2 * per + 2, width, size), BF16),
            in_specs=[VMEM, VMEM],
            out_specs=VMEM,
            compiler_params=params(),
        )(weight, mixed)
        back = lax.all_to_all(back, "cols", 0, 0, tiled=True)

    with jax.named_scope("backward"):
        parts, kept, activated = pl.pallas_call(
            backward_kernel,
            out_shape=(
                jax.ShapeDtypeStruct((peers, SLOTS + 1, width, size), BF16),
                jax.ShapeDtypeStruct((count, width, size), F32),
                jax.ShapeDtypeStruct((width, span), BF16),
            ),
            grid=(steps,),
            in_specs=[SMEM, SMEM, whole(groups, 2 * per + 2, width, size), tile_spec],
            out_specs=(
                whole(peers, SLOTS + 1, width, size),
                whole(count, width, size),
                whole(width, span),
            ),
            scratch_shapes=[
                pltpu.VMEM((STEP, width, size), F32),
                pltpu.VMEM((peers * SLOTS + count, width, size), F32),
            ],
            compiler_params=params(dimension_semantics=("arbitrary",)),
            cost_estimate=cost(2 * tiles * width * size * size, 6 << 20),
        )(place, local, back, tile_vals)
        parts = lax.all_to_all(parts, "rows", 0, 0, tiled=True)

    with jax.named_scope("final"):
        feat_grads, weight_grad = pl.pallas_call(
            functools.partial(final_kernel, float(peers * span) ** -0.5),
            out_shape=(
                jax.ShapeDtypeStruct((width, span), BF16),
                jax.ShapeDtypeStruct((size, width), F32),
            ),
            in_specs=[SMEM, VMEM, VMEM, VMEM],
            out_specs=(VMEM, VMEM),
            scratch_shapes=[
                pltpu.VMEM((count, width, size), F32),
                pltpu.VMEM((count * width, span), BF16),
                pltpu.VMEM((size, span), BF16),
            ],
            compiler_params=params(),
        )(asked, parts, kept, order)
    return activated, feat_grads, weight_grad


def solution(mesh):
    in_specs = (
        P("cols", "rows"),
        P("rows"),
        P("rows"),
        P("rows"),
        P("rows", None, None),
        P(),
        P("cols", "rows"),
    )
    out_specs = (P("cols", "rows"), P("cols", "rows"), P(None, "cols"))
    return jax.shard_map(shards, mesh=mesh, in_specs=in_specs, out_specs=out_specs, check_vma=False)
```

```python
import functools

import jax
import jax.numpy as jnp
from jax import lax
from jax.experimental import pallas as pl
from jax.experimental.pallas import tpu as pltpu
from jax.sharding import PartitionSpec as P

BF16 = jnp.bfloat16
F32 = jnp.float32
I32 = jnp.int32
SLOTS = 8
STEP = 16
WAYS = 2
VMEM = pl.BlockSpec(memory_space=pltpu.VMEM)
SMEM = pl.BlockSpec(memory_space=pltpu.SMEM)
NN = (((1,), (0,)), ((), ()))
NT = (((1,), (1,)), ((), ()))
TN = (((0,), (0,)), ((), ()))


def params(**kw):
    return pltpu.CompilerParams(vmem_limit_bytes=20 << 20, **kw)


def cost(flops, bytes_accessed):
    return pl.CostEstimate(flops=flops, bytes_accessed=bytes_accessed, transcendentals=0)


def dot(a, b, dims):
    return lax.dot_general(a, b, dims, preferred_element_type=F32)


def index_kernel(row_hbm, col_hbm, want_ref, plan_ref, row_buf, col_buf, sems):
    copies = [
        pltpu.make_async_copy(row_hbm, row_buf, sems.at[0]),
        pltpu.make_async_copy(col_hbm, col_buf, sems.at[1]),
    ]
    for c in copies:
        c.start()
    for c in copies:
        c.wait()
    peers = want_ref.shape[0]
    blocks = 32
    col = col_buf[...]
    row = row_buf[...]
    peer, block = col >> 5, col & 31
    tiles = col.shape[1]
    of_peer = (lax.broadcasted_iota(I32, (peers, tiles), 0) == peer).astype(F32)
    of_block = (lax.broadcasted_iota(I32, (blocks, tiles), 0) == block).astype(F32)
    counts = dot(of_peer.astype(BF16), of_block.astype(BF16), NT)
    present = (counts > 0.5).astype(F32)
    before = (
        lax.broadcasted_iota(I32, (blocks, blocks), 0)
        < lax.broadcasted_iota(I32, (blocks, blocks), 1)
    ).astype(F32)
    rank = dot(present.astype(BF16), before.astype(BF16), NN)
    number = lax.broadcasted_iota(I32, (peers, blocks), 1).astype(F32)
    lane = lax.broadcasted_iota(I32, (peers, 128), 1)
    want = jnp.zeros((peers, 128), F32)
    for s in range(SLOTS):
        chosen = jnp.sum(
            jnp.where(rank == float(s), present * number, 0.0), axis=1, keepdims=True
        )
        want = jnp.where(lane == s, chosen, want)
    want_ref[...] = want.astype(I32).reshape(peers, 1, 128)
    rank_of = dot(rank.astype(BF16), of_peer.astype(BF16), TN)
    tile_rank = jnp.sum(rank_of * of_block, axis=0, keepdims=True)
    own = (peer == (row >> 5)).astype(F32)
    block_f, peer_f = block.astype(F32), peer.astype(F32)
    earlier = (
        lax.broadcasted_iota(I32, (tiles, tiles), 0) < lax.broadcasted_iota(I32, (tiles, tiles), 1)
    ).astype(F32)
    both = jnp.concatenate([own, 1.0 - own, jnp.zeros((6, tiles), F32)], axis=0)
    ahead = dot(both.astype(BF16), earlier.astype(BF16), NN)
    own_count = jnp.sum(own, axis=1, keepdims=True)
    spot = jnp.where(own > 0.5, ahead[0:1], own_count + ahead[1:2])
    moved = (lax.broadcasted_iota(I32, (tiles, tiles), 0).astype(F32) == spot).astype(F32)
    tile_f = lax.broadcasted_iota(I32, (1, tiles), 1).astype(F32)
    values = jnp.concatenate(
        [
            tile_f,
            jnp.where(own > 0.5, float(peers), peer_f),
            jnp.where(own > 0.5, block_f, tile_rank),
            (row & 31).astype(F32),
            jnp.zeros((4, tiles), F32),
        ],
        axis=0,
    )
    ordered = dot(values.astype(BF16), moved.astype(BF16), NT)
    place = ordered[1:2] * float(SLOTS) + ordered[2:3]
    plan = jnp.concatenate(
        [
            ordered[0:1],
            place,
            ordered[3:4],
            jnp.broadcast_to(own_count, (1, tiles)),
            jnp.zeros((4, tiles), F32),
        ],
        axis=0,
    )
    plan_ref[...] = plan.astype(I32)


def pick_lanes(blocked, pick, high):
    width = 16
    spread = dot(blocked, pick, NN)
    total = jnp.zeros((width, pick.shape[1]), F32)
    for s in range(blocked.shape[0] // width):
        total = total + jnp.where(high == s, spread[s * width : (s + 1) * width], 0.0)
    return total.astype(BF16)


def permute_kernel(features_ref, order_ref, out_ref, blocked):
    count = order_ref.shape[0]
    width = features_ref.shape[0]
    for s in range(count):
        blocked[s * width : (s + 1) * width, :] = features_ref[:, s * 128 : (s + 1) * 128]
    low = lax.broadcasted_iota(I32, (128, 256), 0)
    for j in range(0, count, 2):
        o = jnp.concatenate([order_ref[j : j + 1, :], order_ref[j + 1 : j + 2, :]], axis=1)
        o = o & (count * 128 - 1)
        pick = jnp.where(low == (o & 127), 1.0, 0.0).astype(BF16)
        total = pick_lanes(blocked[...], pick, o >> 7)
        out_ref[j] = total[:, :128]
        out_ref[j + 1] = total[:, 128:]


def pack_kernel(asked_ref, blocks_ref, send_ref):
    for p in range(send_ref.shape[0]):
        for s in range(SLOTS):
            send_ref[p, s] = blocks_ref[asked_ref[p, 0, s]]


def add_products(plan_ref, first, last, left, tiles_ref, dims, into, spare, prod, total):
    def step(i, carry):
        for u in range(STEP):
            k = i * STEP + u
            prod[u] = dot(left(k), tiles_ref[plan_ref[0, k]], dims)
        for u in range(STEP):
            k = i * STEP + u
            at = jnp.where((k >= first) & (k < last), into(k), spare)
            total[at] = total[at] + prod[u]
        return carry

    lax.fori_loop(first // STEP, (last + STEP - 1) // STEP, step, 0)


def forward_own_kernel(base, plan_ref, own_ref, tiles_ref, out_ref, prod, total):
    count = own_ref.shape[0]
    total[...] = jnp.zeros_like(total)
    add_products(
        plan_ref,
        0,
        plan_ref[3, 0],
        lambda k: own_ref[jnp.maximum(plan_ref[1, k] - base, 0)],
        tiles_ref,
        NT,
        lambda k: plan_ref[2, k],
        count,
        prod,
        total,
    )
    out_ref[...] = total[:count]


def forward_kernel(plan_ref, got_ref, part_ref, grad_ref, tiles_ref, out_ref, prod, total):
    groups = out_ref.shape[0]
    per = out_ref.shape[1] // 2
    count = part_ref.shape[0]
    slots = got_ref.shape[0]
    total[:count] = part_ref[...]
    add_products(
        plan_ref,
        plan_ref[3, 0],
        tiles_ref.shape[0],
        lambda k: got_ref[jnp.minimum(plan_ref[1, k], slots - 1)],
        tiles_ref,
        NT,
        lambda k: plan_ref[2, k],
        count,
        prod,
        total,
    )
    for c in range(groups):
        for b in range(per):
            at = (c * per + b) * 128
            out_ref[c, b] = total[c * per + b].astype(BF16)
            out_ref[c, per + b] = grad_ref[:, at : at + 128]


def dense_kernel(weight_ref, got_ref, out_ref):
    groups, _, width, _ = got_ref.shape
    per = got_ref.shape[1] // 2
    inputs = groups * width
    weight = weight_ref[...]
    weight_t = weight.astype(F32).T.astype(BF16)
    part = jnp.zeros((inputs, inputs), F32)
    for b in range(per):
        agg = got_ref[:, b].reshape(inputs, 128)
        grad = got_ref[:, per + b].reshape(inputs, 128).astype(F32)
        pre = dot(weight_t, agg, NN)
        logistic = jax.nn.sigmoid(pre)
        act = (pre * logistic).astype(BF16)
        pre_grad = (grad * logistic * (1.0 + pre * (1.0 - logistic))).astype(BF16)
        agg_grad = dot(weight, pre_grad, NN).astype(BF16)
        part = part + dot(pre_grad, agg, NT)
        out_ref[:, b] = agg_grad.reshape(groups, width, 128)
        out_ref[:, per + b] = act.reshape(groups, width, 128)
    high = part.astype(BF16)
    out_ref[:, 2 * per] = high.reshape(groups, width, 128)
    out_ref[:, 2 * per + 1] = (part - high.astype(F32)).astype(BF16).reshape(groups, width, 128)


def backward_kernel(plan_ref, got_ref, tiles_ref, send_ref, prod, total):
    groups = got_ref.shape[0]
    per = (got_ref.shape[1] - 2) // 2
    peers = send_ref.shape[0]
    slots = peers * SLOTS
    total[...] = jnp.zeros_like(total)
    add_products(
        plan_ref,
        plan_ref[3, 0],
        tiles_ref.shape[0],
        lambda k: got_ref[plan_ref[2, k] // per, plan_ref[2, k] % per],
        tiles_ref,
        NN,
        lambda k: jnp.minimum(plan_ref[1, k], slots),
        slots,
        prod,
        total,
    )
    part = got_ref[0, 2 * per].astype(F32) + got_ref[0, 2 * per + 1].astype(F32)
    for c in range(1, groups):
        part = part + got_ref[c, 2 * per].astype(F32) + got_ref[c, 2 * per + 1].astype(F32)
    part = part.astype(BF16)
    for p in range(peers):
        send_ref[p, :SLOTS] = total[p * SLOTS : (p + 1) * SLOTS].astype(BF16)
        send_ref[p, SLOTS] = part


def backward_own_kernel(base, plan_ref, got_ref, tiles_ref, order_ref, out_ref, act_ref, inverse_ref, pick_ref, prod, total, spots):
    count, width = out_ref.shape[:2]
    groups = got_ref.shape[0]
    per = (got_ref.shape[1] - 2) // 2
    total[...] = jnp.zeros_like(total)
    add_products(
        plan_ref,
        0,
        plan_ref[3, 0],
        lambda k: got_ref[plan_ref[2, k] // per, plan_ref[2, k] % per],
        tiles_ref,
        NN,
        lambda k: jnp.maximum(plan_ref[1, k] - base, 0),
        count,
        prod,
        total,
    )
    out_ref[...] = total[:count]
    for c in range(groups):
        for b in range(per):
            at = (c * per + b) * 128
            act_ref[:, at : at + 128] = got_ref[c, per + b]
    low = lax.broadcasted_iota(I32, (128, 128), 0)
    source = lax.broadcasted_iota(I32, (count, 128), 0)
    lane = lax.broadcasted_iota(I32, (count, 128), 1).astype(F32)
    for j in range(count):
        o = order_ref[j : j + 1, :] & (count * 128 - 1)
        lanes = slice(j * 128, (j + 1) * 128)
        pick_ref[:, lanes] = jnp.where(low == (o & 127), 1.0, 0.0).astype(BF16)
        here = source == (o >> 7)
        spots[:count, lanes] = jnp.where(here, float(j), 0.0).astype(BF16)
        spots[count:, lanes] = jnp.where(here, lane, 0.0).astype(BF16)
    inverse = dot(spots[...], pick_ref[...], NT).astype(I32)
    inverse_ref[...] = inverse[:count]
    for j in range(count):
        pick_ref[:, j * 128 : (j + 1) * 128] = jnp.where(
            low == inverse[count + j : count + j + 1, :], 1.0, 0.0
        ).astype(BF16)


def final_kernel(scale, asked_ref, got_ref, own_ref, inverse_ref, pick_ref, grads_ref, weight_ref, *totals):
    peers = got_ref.shape[0]
    count, width = own_ref.shape[:2]
    ways = len(totals)
    for w, total in enumerate(totals):
        total[...] = own_ref[...] if w == 0 else jnp.zeros_like(total)
    part = got_ref[0, SLOTS].astype(F32)
    for p in range(1, peers):
        part = part + got_ref[p, SLOTS].astype(F32)
    weight_ref[...] = part * scale
    for p in range(0, peers, ways):
        for s in range(SLOTS):
            for w, total in enumerate(totals):
                at = asked_ref[p + w, 0, s]
                total[at] = total[at] + got_ref[p + w, s].astype(F32)
    node = totals[0][...]
    for total in totals[1:]:
        node = node + total[...]
    blocked = node.astype(BF16).reshape(count * width, 128)
    for j in range(0, count, 2):
        high = jnp.concatenate([inverse_ref[j : j + 1, :], inverse_ref[j + 1 : j + 2, :]], axis=1)
        lanes = slice(j * 128, (j + 2) * 128)
        grads_ref[:, lanes] = pick_lanes(blocked, pick_ref[:, lanes], high)


def shards(features, node_order, tile_row, tile_col, tile_vals, weight, grad_out):
    width, span = features.shape
    tiles, size, _ = tile_vals.shape
    count = span // size
    peers = lax.axis_size("rows")
    groups = lax.axis_size("cols")
    per = count // groups
    order = node_order.reshape(count, size)
    shape = jax.ShapeDtypeStruct
    prod = pltpu.VMEM((STEP, width, size), F32)
    sums = lambda n: pltpu.VMEM((n + 1, width, size), F32)

    with jax.named_scope("index"):
        want, plan = pl.pallas_call(
            index_kernel,
            out_shape=(shape((peers, 1, 128), I32), shape((8, tiles), I32)),
            in_specs=[pl.BlockSpec(memory_space=pltpu.HBM)] * 2,
            out_specs=(VMEM, VMEM),
            scratch_shapes=[
                pltpu.VMEM((1, tiles), I32),
                pltpu.VMEM((1, tiles), I32),
                pltpu.SemaphoreType.DMA((2,)),
            ],
            compiler_params=params(),
        )(tile_row.reshape(1, tiles), tile_col.reshape(1, tiles))
        asked = lax.all_to_all(want, "rows", 0, 0, tiled=True)

    with jax.named_scope("permute"):
        own = pl.pallas_call(
            permute_kernel,
            out_shape=shape((count, width, size), BF16),
            in_specs=[VMEM, VMEM],
            out_specs=VMEM,
            scratch_shapes=[pltpu.VMEM((count * width, size), BF16)],
            compiler_params=params(),
            cost_estimate=cost(1 << 31, 1 << 22),
        )(features, order)

    with jax.named_scope("pack"):
        send = pl.pallas_call(
            pack_kernel,
            out_shape=shape((peers, SLOTS, width, size), BF16),
            in_specs=[SMEM, VMEM],
            out_specs=VMEM,
            compiler_params=params(),
        )(asked, own)
        got = lax.all_to_all(send, "rows", 0, 0, tiled=True)

    with jax.named_scope("forward_own"):
        part = pl.pallas_call(
            functools.partial(forward_own_kernel, peers * SLOTS),
            out_shape=shape((count, width, size), F32),
            in_specs=[SMEM, VMEM, VMEM],
            out_specs=VMEM,
            scratch_shapes=[prod, sums(count)],
            compiler_params=params(),
            cost_estimate=cost(1 << 31, 1 << 22),
        )(plan, own, tile_vals)

    with jax.named_scope("forward"):
        mixed = pl.pallas_call(
            forward_kernel,
            out_shape=shape((groups, 2 * per, width, size), BF16),
            in_specs=[SMEM, VMEM, VMEM, VMEM, VMEM],
            out_specs=VMEM,
            scratch_shapes=[prod, sums(count)],
            compiler_params=params(),
            cost_estimate=cost(1 << 30, 1 << 22),
        )(plan, got.reshape(peers * SLOTS, width, size), part, grad_out, tile_vals)
        mixed = lax.all_to_all(mixed, "cols", 0, 0, tiled=True)

    with jax.named_scope("dense"):
        back = pl.pallas_call(
            dense_kernel,
            out_shape=shape((groups, 2 * per + 2, width, size), BF16),
            in_specs=[VMEM, VMEM],
            out_specs=VMEM,
            compiler_params=params(),
        )(weight, mixed)
        back = lax.all_to_all(back, "cols", 0, 0, tiled=True)

    with jax.named_scope("backward"):
        parts = pl.pallas_call(
            backward_kernel,
            out_shape=shape((peers, SLOTS + 1, width, size), BF16),
            in_specs=[SMEM, VMEM, VMEM],
            out_specs=VMEM,
            scratch_shapes=[prod, sums(peers * SLOTS)],
            compiler_params=params(),
            cost_estimate=cost(1 << 30, 1 << 22),
        )(plan, back, tile_vals)
        parts = lax.all_to_all(parts, "rows", 0, 0, tiled=True)

    with jax.named_scope("backward_own"):
        kept, activated, inverse, pick = pl.pallas_call(
            functools.partial(backward_own_kernel, peers * SLOTS),
            out_shape=(
                shape((count, width, size), F32),
                shape((width, span), BF16),
                shape((count, size), I32),
                shape((size, span), BF16),
            ),
            in_specs=[SMEM, VMEM, VMEM, VMEM],
            out_specs=(VMEM, VMEM, VMEM, VMEM),
            scratch_shapes=[prod, sums(count), pltpu.VMEM((2 * count, span), BF16)],
            compiler_params=params(),
            cost_estimate=cost(1 << 31, 1 << 22),
        )(plan, back, tile_vals, order)

    with jax.named_scope("final"):
        feat_grads, weight_grad = pl.pallas_call(
            functools.partial(final_kernel, float(peers * span) ** -0.5),
            out_shape=(shape((width, span), BF16), shape((width, size), F32)),
            in_specs=[SMEM, VMEM, VMEM, VMEM, VMEM],
            out_specs=(VMEM, VMEM),
            scratch_shapes=[pltpu.VMEM((count, width, size), F32)] * WAYS,
            compiler_params=params(),
        )(asked, parts, kept, inverse, pick)
    return activated, feat_grads, weight_grad.T


def solution(mesh):
    in_specs = (
        P("cols", "rows"),
        P("rows"),
        P("rows"),
        P("rows"),
        P("rows", None, None),
        P(),
        P("cols", "rows"),
    )
    out_specs = (P("cols", "rows"), P("cols", "rows"), P(None, "cols"))
    return jax.shard_map(shards, mesh=mesh, in_specs=in_specs, out_specs=out_specs, check_vma=False)
```

```python
import functools

import jax
import jax.numpy as jnp
from jax import lax
from jax.experimental import pallas as pl
from jax.experimental.pallas import tpu as pltpu
from jax.sharding import PartitionSpec as P

BF16 = jnp.bfloat16
F32 = jnp.float32
I32 = jnp.int32
SLOTS = 8
STEP = 16
WAYS = 4
PIECES = 8
VMEM = pl.BlockSpec(memory_space=pltpu.VMEM)
HBM = pl.BlockSpec(memory_space=pltpu.HBM)
SMEM = pl.BlockSpec(memory_space=pltpu.SMEM)
NN = (((1,), (0,)), ((), ()))
NT = (((1,), (1,)), ((), ()))
TN = (((0,), (0,)), ((), ()))


def params(**kw):
    return pltpu.CompilerParams(vmem_limit_bytes=20 << 20, **kw)


def cost(flops, bytes_accessed):
    return pl.CostEstimate(flops=flops, bytes_accessed=bytes_accessed, transcendentals=0)


def send_out(buf, out_hbm, sems, piece):
    size = buf.shape[0] // sems.shape[0]
    at = pl.ds(piece * size, size)
    return pltpu.make_async_copy(buf.at[at], out_hbm.at[at], sems.at[piece])


def over_cols(value, here):
    groups = value.shape[0]
    rings = groups // 2
    value = value.reshape(rings, 2, *value.shape[1:])
    core, ring = here % 2, here // 2
    kept = lax.dynamic_index_in_dim(value, core, 1, keepdims=False)
    passed = lax.dynamic_index_in_dim(value, 1 - core, 1, keepdims=False)
    passed = lax.ppermute(passed, "cols", [(i, i ^ 1) for i in range(groups)])
    both = jnp.stack([kept, passed], axis=1)
    parts = []
    for far in range(rings):
        part = lax.dynamic_index_in_dim(both, (ring + far) % rings, 0, keepdims=False)
        if far:
            pairs = [(i, (i + 2 * far) % groups) for i in range(groups)]
            part = lax.ppermute(part, "cols", pairs)
        parts.append(part)
    return jnp.stack(parts)


def in_hbm(x):
    return pltpu.with_memory_space_constraint(x, pltpu.HBM)


def dot(a, b, dims):
    return lax.dot_general(a, b, dims, preferred_element_type=F32)


def ranks(col, peers):
    peer, block = col >> 5, col & 31
    of_peer = (lax.broadcasted_iota(I32, (peers, col.shape[1]), 0) == peer).astype(F32)
    of_block = (lax.broadcasted_iota(I32, (32, col.shape[1]), 0) == block).astype(F32)
    counts = dot(of_peer.astype(BF16), of_block.astype(BF16), NT)
    present = (counts > 0.5).astype(F32)
    before = lower(32).astype(F32)
    return of_peer, of_block, present, dot(present.astype(BF16), before.astype(BF16), NN)


def lower(n):
    return lax.broadcasted_iota(I32, (n, n), 0) < lax.broadcasted_iota(I32, (n, n), 1)


def want_kernel(col_hbm, want_ref, col_buf, sem):
    copy = pltpu.make_async_copy(col_hbm, col_buf, sem)
    copy.start()
    copy.wait()
    peers = want_ref.shape[0]
    _, _, present, rank = ranks(col_buf[...], peers)
    number = lax.broadcasted_iota(I32, (peers, 32), 1).astype(F32)
    lane = lax.broadcasted_iota(I32, (peers, 128), 1)
    want = jnp.zeros((peers, 128), F32)
    for s in range(SLOTS):
        chosen = jnp.sum(
            jnp.where(rank == float(s), present * number, 0.0), axis=1, keepdims=True
        )
        want = jnp.where(lane == s, chosen, want)
    want_ref[...] = want.astype(I32).reshape(peers, 1, 128)


def plan_kernel(peers, row_ref, col_ref, plan_ref):
    col, row = col_ref[...], row_ref[...]
    tiles = col.shape[1]
    of_peer, of_block, _, rank = ranks(col, peers)
    rank_of = dot(rank.astype(BF16), of_peer.astype(BF16), TN)
    tile_rank = jnp.sum(rank_of * of_block, axis=0, keepdims=True)
    own = ((col >> 5) == (row >> 5)).astype(F32)
    own_count = jnp.sum(own, axis=1, keepdims=True)
    earlier = lower(tiles).astype(F32).astype(BF16)
    far_peer = of_peer * (1.0 - own)
    same = dot(far_peer.astype(BF16), earlier, NN)
    totals = jnp.sum(far_peer, axis=1, keepdims=True)
    upper = (
        lax.broadcasted_iota(I32, (peers, peers), 0) > lax.broadcasted_iota(I32, (peers, peers), 1)
    ).astype(F32)
    wide = jnp.broadcast_to(totals, (peers, tiles))
    starts = dot(upper.astype(BF16), wide.astype(BF16), NN)
    ahead = jnp.sum(far_peer * (same + starts), axis=0, keepdims=True)
    own_ahead = dot(jnp.broadcast_to(own, (8, tiles)).astype(BF16), earlier, NN)[0:1]
    spot = jnp.where(own > 0.5, own_ahead, own_count + ahead)
    moved = (lax.broadcasted_iota(I32, (tiles, tiles), 0).astype(F32) == spot).astype(F32)
    values = jnp.concatenate(
        [
            lax.broadcasted_iota(I32, (1, tiles), 1).astype(F32),
            jnp.where(own > 0.5, float(peers), (col >> 5).astype(F32)),
            jnp.where(own > 0.5, (col & 31).astype(F32), tile_rank),
            (row & 31).astype(F32),
            jnp.zeros((4, tiles), F32),
        ],
        axis=0,
    )
    ordered = dot(values.astype(BF16), moved.astype(BF16), NT)
    lanes = lax.broadcasted_iota(I32, (peers, tiles), 1)
    diagonal = (lanes == lax.broadcasted_iota(I32, (peers, tiles), 0)).astype(F32)
    firsts = own_count + jnp.sum(starts * diagonal, axis=0, keepdims=True)
    plan = jnp.concatenate(
        [
            ordered[0:1],
            ordered[1:2] * float(SLOTS) + ordered[2:3],
            ordered[3:4],
            jnp.broadcast_to(own_count, (1, tiles)),
            firsts,
            jnp.zeros((3, tiles), F32),
        ],
        axis=0,
    )
    plan_ref[...] = plan.astype(I32)


def pick_lanes(blocked, pick, high):
    width = 16
    spread = dot(blocked, pick, NN)
    total = jnp.zeros((width, pick.shape[1]), F32)
    for s in range(blocked.shape[0] // width):
        total = total + jnp.where(high == s, spread[s * width : (s + 1) * width], 0.0)
    return total.astype(BF16)


def permute_kernel(features_ref, order_ref, out_ref, blocked):
    count = order_ref.shape[0]
    width = features_ref.shape[0]
    for s in range(count):
        blocked[s * width : (s + 1) * width, :] = features_ref[:, s * 128 : (s + 1) * 128]
    low = lax.broadcasted_iota(I32, (128, 256), 0)
    for j in range(0, count, 2):
        o = jnp.concatenate([order_ref[j : j + 1, :], order_ref[j + 1 : j + 2, :]], axis=1)
        o = o & (count * 128 - 1)
        pick = jnp.where(low == (o & 127), 1.0, 0.0).astype(BF16)
        total = pick_lanes(blocked[...], pick, o >> 7)
        out_ref[j] = total[:, :128]
        out_ref[j + 1] = total[:, 128:]


def pack_kernel(asked_ref, blocks_ref, buf):
    for p in range(buf.shape[0]):
        for s in range(SLOTS):
            buf[p, s] = blocks_ref[asked_ref[p, 0, s]]


def chunk_copy(tiles_hbm, tiles, sems, i):
    at = pl.ds(i * STEP, STEP)
    return pltpu.make_async_copy(tiles_hbm.at[at], tiles.at[at], sems.at[i])


def fetch_tiles(first, last, tiles_hbm, tiles, sems):
    def start(i, carry):
        chunk_copy(tiles_hbm, tiles, sems, i).start()
        return carry

    lax.fori_loop(first, last, start, 0)


def add_products(plan_ref, first, last, left, tile, dims, into, spare, prod, total, arrive=None):
    def step(i, carry):
        if arrive is not None:
            arrive(i)
        for u in range(STEP):
            k = i * STEP + u
            prod[u] = dot(left(k), tile(k), dims)
        for u in range(STEP):
            k = i * STEP + u
            at = jnp.where((k >= first) & (k < last), into(k), spare)
            total[at] = total[at] + prod[u]
        return carry

    lax.fori_loop(first // STEP, (last + STEP - 1) // STEP, step, 0)


def forward_own_kernel(base, plan_ref, own_ref, tiles_hbm, out_ref, list_hbm, prod, total, tiles, sem, out_sem):
    count = own_ref.shape[0]
    for k in range(tiles.shape[0]):
        pltpu.make_async_copy(tiles_hbm.at[plan_ref[0, k]], tiles.at[k], sem).start()
    pltpu.make_async_copy(tiles_hbm, tiles, sem).wait()
    store = pltpu.make_async_copy(tiles, list_hbm, out_sem)
    store.start()
    total[...] = jnp.zeros_like(total)
    add_products(
        plan_ref,
        0,
        plan_ref[3, 0],
        lambda k: own_ref[jnp.maximum(plan_ref[1, k] - base, 0)],
        lambda k: tiles[k],
        NT,
        lambda k: plan_ref[2, k],
        count,
        prod,
        total,
    )
    out_ref[...] = total[:count]
    store.wait()


def forward_kernel(plan_ref, got_ref, part_ref, tiles_hbm, out_ref, prod, total, tiles, sems):
    first = plan_ref[3, 0]

    fetch_tiles(first // STEP, tiles.shape[0] // STEP, tiles_hbm, tiles, sems)
    groups, per = out_ref.shape[:2]
    count = part_ref.shape[0]
    slots = got_ref.shape[0]
    total[:count] = part_ref[...]
    add_products(
        plan_ref,
        first,
        tiles.shape[0],
        lambda k: got_ref[jnp.minimum(plan_ref[1, k], slots - 1)],
        lambda k: tiles[k],
        NT,
        lambda k: plan_ref[2, k],
        count,
        prod,
        total,
        lambda i: chunk_copy(tiles_hbm, tiles, sems, i).wait(),
    )
    for c in range(groups):
        for b in range(per):
            out_ref[c, b] = total[c * per + b].astype(BF16)


def source(here, far, core):
    rings = 4
    y, c = here // 2, here % 2
    return (y + rings - far) % rings * 2 + (c + core) % 2


def dense_kernel(here_ref, weight_ref, got_ref, grad_ref, out_ref, act_hbm, grads, act_ref, sems):
    groups, per, width, _ = got_ref.shape
    for far in range(groups // 2):
        for core in range(2):
            grads[source(here_ref[0], far, core)] = grad_ref[far, core]
    inputs = groups * width
    weight = weight_ref[...]
    weight_t = weight.astype(F32).T.astype(BF16)
    part = jnp.zeros((inputs, inputs), F32)
    stores = []
    for b in range(per):
        agg = got_ref[:, b].reshape(inputs, 128)
        grad = grads[:, b].reshape(inputs, 128).astype(F32)
        pre = dot(weight_t, agg, NN)
        logistic = jax.nn.sigmoid(pre)
        act = (pre * logistic).astype(BF16)
        pre_grad = (grad * logistic * (1.0 + pre * (1.0 - logistic))).astype(BF16)
        agg_grad = dot(weight, pre_grad, NN).astype(BF16)
        part = part + dot(pre_grad, agg, NT)
        out_ref[:, b] = agg_grad.reshape(groups, width, 128)
        act_ref[:, b] = act.reshape(groups, width, 128)
        store = pltpu.make_async_copy(act_ref.at[:, b], act_hbm.at[:, b], sems.at[b])
        store.start()
        stores.append(store)
    high = part.astype(BF16)
    out_ref[:, per] = high.reshape(groups, width, 128)
    out_ref[:, per + 1] = (part - high.astype(F32)).astype(BF16).reshape(groups, width, 128)
    for store in stores:
        store.wait()


def backward_kernel(plan_ref, got_ref, tiles_hbm, send_hbm, prod, total, buf, sems, tiles, tile_sems):
    last = tiles.shape[0] // STEP
    begin = jnp.minimum(plan_ref[3, 0] // STEP, last - 1)

    fetch_tiles(begin, last, tiles_hbm, tiles, tile_sems)
    groups = got_ref.shape[0]
    per = got_ref.shape[1] - 2
    peers = buf.shape[0]
    pieces = sems.shape[0]
    share = peers // pieces
    slots = peers * SLOTS
    total[...] = jnp.zeros_like(total)
    part = got_ref[0, per].astype(F32) + got_ref[0, per + 1].astype(F32)
    for c in range(1, groups):
        part = part + got_ref[c, per].astype(F32) + got_ref[c, per + 1].astype(F32)
    part = part.astype(BF16)
    for p in range(peers):
        buf[p, SLOTS] = part

    def step(i, carry):
        chunk_copy(tiles_hbm, tiles, tile_sems, i).wait()
        for u in range(STEP):
            r = plan_ref[2, i * STEP + u]
            prod[u] = dot(got_ref[r // per, r % per], tiles[i * STEP + u], NN)
        for u in range(STEP):
            k = i * STEP + u
            at = jnp.where(k >= plan_ref[3, 0], jnp.minimum(plan_ref[1, k], slots), slots)
            total[at] = total[at] + prod[u]
        done = (i + 1) * STEP
        for piece in range(pieces):
            until = plan_ref[4, (piece + 1) * share] if piece + 1 < pieces else last * STEP

            @pl.when((until <= done) & ((until > i * STEP) | (i == begin)))
            def _():
                for p in range(piece * share, (piece + 1) * share):
                    buf[p, :SLOTS] = total[p * SLOTS : (p + 1) * SLOTS].astype(BF16)
                send_out(buf, send_hbm, sems, piece).start()

        return carry

    lax.fori_loop(begin, last, step, 0)
    for piece in range(pieces):
        send_out(buf, send_hbm, sems, piece).wait()


def backward_own_kernel(
    base, plan_ref, got_ref, tiles_hbm, order_ref, asked_ref, out_hbm, inverse_ref, pick_ref, flat_ref, prod, total, tiles, sems, spots, low_pick, out_sem
):
    fetch_tiles(0, (plan_ref[3, 0] + STEP - 1) // STEP, tiles_hbm, tiles, sems)
    count, width = out_hbm.shape[:2]
    per = got_ref.shape[1] - 2
    total[...] = jnp.zeros_like(total)
    add_products(
        plan_ref,
        0,
        plan_ref[3, 0],
        lambda k: got_ref[plan_ref[2, k] // per, plan_ref[2, k] % per],
        lambda k: tiles[k],
        NN,
        lambda k: jnp.maximum(plan_ref[1, k] - base, 0),
        count,
        prod,
        total,
        lambda i: chunk_copy(tiles_hbm, tiles, sems, i).wait(),
    )
    store = pltpu.make_async_copy(total.at[pl.ds(0, count)], out_hbm, out_sem)
    store.start()
    low = lax.broadcasted_iota(I32, (128, 128), 0)
    source = lax.broadcasted_iota(I32, (count, 128), 0)
    lane = lax.broadcasted_iota(I32, (count, 128), 1).astype(F32)
    for j in range(count):
        o = order_ref[j : j + 1, :] & (count * 128 - 1)
        lanes = slice(j * 128, (j + 1) * 128)
        low_pick[:, lanes] = jnp.where(low == (o & 127), 1.0, 0.0).astype(BF16)
        here = source == (o >> 7)
        spots[:count, lanes] = jnp.where(here, float(j), 0.0).astype(BF16)
        spots[count:, lanes] = jnp.where(here, lane, 0.0).astype(BF16)
    inverse = dot(spots[...], low_pick[...], NT).astype(I32)
    odd = lax.broadcasted_iota(I32, (256, 128), 0)
    for j in range(count):
        at = inverse[count + j : count + j + 1, :] + (inverse[j : j + 1, :] & 1) * 128
        pick_ref[:, j * 128 : (j + 1) * 128] = jnp.where(odd == at, 1.0, 0.0).astype(BF16)
    inverse_ref[...] = inverse[:count] >> 1
    peers = asked_ref.shape[0]
    spread = dot(
        asked_ref[...].reshape(peers, 128).astype(F32).astype(BF16),
        (
            lax.broadcasted_iota(I32, (128, 256), 0) == lax.broadcasted_iota(I32, (128, 256), 1) % SLOTS
        ).astype(F32).astype(BF16),
        NN,
    )
    mine = lax.broadcasted_iota(I32, (peers, 256), 0) == lax.broadcasted_iota(I32, (peers, 256), 1) // SLOTS
    flat_ref[...] = jnp.sum(jnp.where(mine, spread, 0.0), axis=0, keepdims=True).astype(I32)
    store.wait()


def blocks_kernel(grad_ref, out_ref):
    groups, per = out_ref.shape[:2]
    for c in range(groups):
        for b in range(per):
            at = (c * per + b) * 128
            out_ref[c, b] = grad_ref[:, at : at + 128]


def lanes_kernel(here_ref, got_ref, out_ref):
    for far in range(got_ref.shape[0]):
        for core in range(2):
            at = source(here_ref[0], far, core) * got_ref.shape[2]
            for b in range(got_ref.shape[2]):
                out_ref[:, pl.ds(pl.multiple_of((at + b) * 128, 128), 128)] = got_ref[far, core, b]


def final_kernel(scale, asked_ref, got_ref, own_hbm, inverse_ref, pick_ref, grads_ref, weight_ref, own, sem, *totals):
    fetch = pltpu.make_async_copy(own_hbm, own, sem)
    fetch.start()
    peers = got_ref.shape[0]
    count, width = own.shape[:2]
    ways = len(totals)
    for total in totals:
        total[...] = jnp.zeros_like(total)
    part = got_ref[0, SLOTS].astype(F32)
    for p in range(1, peers):
        part = part + got_ref[p, SLOTS].astype(F32)
    weight_ref[...] = part * scale
    for p in range(0, peers, ways):
        for s in range(SLOTS):
            for w, total in enumerate(totals):
                at = asked_ref[0, (p + w) * SLOTS + s]
                total[at] = total[at] + got_ref[p + w, s].astype(F32)
    fetch.wait()
    node = own[...]
    for total in totals:
        node = node + total[...]
    node = node.astype(BF16)
    blocked = jnp.concatenate(
        [jnp.concatenate([node[j], node[j + 1]], axis=1) for j in range(0, count, 2)], axis=0
    )
    for j in range(0, count, 2):
        high = jnp.concatenate([inverse_ref[j : j + 1, :], inverse_ref[j + 1 : j + 2, :]], axis=1)
        lanes = slice(j * 128, (j + 2) * 128)
        grads_ref[:, lanes] = pick_lanes(blocked, pick_ref[:, lanes], high)


def shards(features, node_order, tile_row, tile_col, tile_vals, weight, grad_out):
    width, span = features.shape
    tiles, size, _ = tile_vals.shape
    count = span // size
    peers = lax.axis_size("rows")
    groups = lax.axis_size("cols")
    per = count // groups
    order = node_order.reshape(count, size)
    shape = jax.ShapeDtypeStruct
    prod = pltpu.VMEM((STEP, width, size), F32)
    tile_buf = pltpu.VMEM(tile_vals.shape, BF16)
    sums = lambda n: pltpu.VMEM((n + 1, width, size), F32)

    with jax.named_scope("index"):
        rows, cols = tile_row.reshape(1, tiles), tile_col.reshape(1, tiles)
        want = pl.pallas_call(
            want_kernel,
            out_shape=shape((peers, 1, 128), I32),
            in_specs=[HBM],
            out_specs=VMEM,
            scratch_shapes=[pltpu.VMEM((1, tiles), I32), pltpu.SemaphoreType.DMA],
            compiler_params=params(),
        )(in_hbm(cols))
        asked = lax.all_to_all(want, "rows", 0, 0, tiled=True)
        plan = pl.pallas_call(
            functools.partial(plan_kernel, peers),
            out_shape=shape((8, tiles), I32),
            in_specs=[VMEM, VMEM],
            out_specs=VMEM,
            compiler_params=params(),
            cost_estimate=cost(1 << 30, 1 << 21),
        )(rows, cols)

    with jax.named_scope("permute"):
        own = pl.pallas_call(
            permute_kernel,
            out_shape=shape((count, width, size), BF16),
            in_specs=[VMEM, VMEM],
            out_specs=VMEM,
            scratch_shapes=[pltpu.VMEM((count * width, size), BF16)],
            compiler_params=params(),
            cost_estimate=cost(1 << 31, 1 << 22),
        )(features, order)

    with jax.named_scope("pack"):
        send = pl.pallas_call(
            pack_kernel,
            out_shape=pltpu.VMEM((peers, SLOTS, width, size), BF16),
            in_specs=[SMEM, VMEM],
            out_specs=VMEM,
            compiler_params=params(),
        )(asked, own)
        got = lax.all_to_all(send, "rows", 0, 0, tiled=True)

    with jax.named_scope("forward_own"):
        part, tile_list = pl.pallas_call(
            functools.partial(forward_own_kernel, peers * SLOTS),
            out_shape=(shape((count, width, size), F32), pltpu.HBM(tile_vals.shape, BF16)),
            in_specs=[SMEM, VMEM, HBM],
            out_specs=(VMEM, HBM),
            scratch_shapes=[prod, sums(count), tile_buf, pltpu.SemaphoreType.DMA, pltpu.SemaphoreType.DMA],
            compiler_params=params(),
            cost_estimate=cost(1 << 31, 1 << 22),
        )(plan, own, in_hbm(tile_vals))

    with jax.named_scope("grads"):
        here = lax.axis_index("cols")
        grad_out, part = lax.optimization_barrier((grad_out, part))
        grads = pl.pallas_call(
            blocks_kernel,
            out_shape=shape((groups, per, width, size), BF16),
            in_specs=[VMEM],
            out_specs=VMEM,
            compiler_params=params(),
        )(grad_out)
        grads, part = lax.optimization_barrier((over_cols(grads, here), part))
        here_at = here.reshape(1)

    with jax.named_scope("forward"):
        mixed = pl.pallas_call(
            forward_kernel,
            out_shape=shape((groups, per, width, size), BF16),
            in_specs=[SMEM, VMEM, VMEM, HBM],
            out_specs=VMEM,
            scratch_shapes=[prod, sums(count), tile_buf, pltpu.SemaphoreType.DMA((tiles // STEP,))],
            compiler_params=params(),
            cost_estimate=cost(1 << 30, 1 << 22),
        )(plan, got.reshape(peers * SLOTS, width, size), part, in_hbm(tile_list))
        mixed = lax.all_to_all(mixed, "cols", 0, 0, tiled=True)

    with jax.named_scope("dense"):
        back, act = pl.pallas_call(
            dense_kernel,
            out_shape=(
                shape((groups, per + 2, width, size), BF16),
                pltpu.HBM((groups, per, width, size), BF16),
            ),
            in_specs=[SMEM, VMEM, VMEM, VMEM],
            out_specs=(VMEM, HBM),
            scratch_shapes=[pltpu.VMEM((groups, per, width, size), BF16)] * 2
            + [pltpu.SemaphoreType.DMA((per,))],
            compiler_params=params(),
        )(here_at, weight, mixed, grads)
        back = lax.all_to_all(back, "cols", 0, 0, tiled=True)

    with jax.named_scope("backward"):
        parts = pl.pallas_call(
            backward_kernel,
            out_shape=shape((peers, SLOTS + 1, width, size), BF16),
            in_specs=[SMEM, VMEM, HBM],
            out_specs=HBM,
            scratch_shapes=[
                prod,
                sums(peers * SLOTS),
                pltpu.VMEM((peers, SLOTS + 1, width, size), BF16),
                pltpu.SemaphoreType.DMA((min(4, peers),)),
                tile_buf,
                pltpu.SemaphoreType.DMA((tiles // STEP,)),
            ],
            compiler_params=params(),
            cost_estimate=cost(1 << 30, 1 << 22),
        )(plan, back, in_hbm(tile_list))
        parts = lax.all_to_all(parts, "rows", 0, 0, tiled=True)

    with jax.named_scope("backward_own"):
        kept, inverse, pick, flat = pl.pallas_call(
            functools.partial(backward_own_kernel, peers * SLOTS),
            out_shape=(
                pltpu.HBM((count, width, size), F32),
                shape((count, size), I32),
                shape((2 * size, span), BF16),
                shape((1, 256), I32),
            ),
            in_specs=[SMEM, VMEM, HBM, VMEM, VMEM],
            out_specs=(HBM, VMEM, VMEM, VMEM),
            scratch_shapes=[
                prod,
                sums(count),
                tile_buf,
                pltpu.SemaphoreType.DMA((tiles // STEP,)),
                pltpu.VMEM((2 * count, span), BF16),
                pltpu.VMEM((size, span), BF16),
                pltpu.SemaphoreType.DMA,
            ],
            compiler_params=params(),
            cost_estimate=cost(1 << 31, 1 << 22),
        )(plan, back, in_hbm(tile_list), order, asked)

    with jax.named_scope("activated"):
        act, kept = lax.optimization_barrier((act, kept))
        activated = pl.pallas_call(
            lanes_kernel,
            out_shape=shape((width, span), BF16),
            in_specs=[SMEM, VMEM],
            out_specs=VMEM,
            compiler_params=params(),
        )(here_at, over_cols(act, here))

    with jax.named_scope("final"):
        feat_grads, weight_grad = pl.pallas_call(
            functools.partial(final_kernel, float(peers * span) ** -0.5),
            out_shape=(shape((width, span), BF16), shape((width, size), F32)),
            in_specs=[SMEM, VMEM, HBM, VMEM, VMEM],
            out_specs=(VMEM, VMEM),
            scratch_shapes=[pltpu.VMEM((count, width, size), F32), pltpu.SemaphoreType.DMA]
            + [pltpu.VMEM((count, width, size), F32)] * WAYS,
            compiler_params=params(),
        )(flat, parts, in_hbm(kept), inverse, pick)
    return activated, feat_grads, weight_grad.T


def solution(mesh):
    in_specs = (
        P("cols", "rows"),
        P("rows"),
        P("rows"),
        P("rows"),
        P("rows", None, None),
        P(),
        P("cols", "rows"),
    )
    out_specs = (P("cols", "rows"), P("cols", "rows"), P(None, "cols"))
    return jax.shard_map(shards, mesh=mesh, in_specs=in_specs, out_specs=out_specs, check_vma=False)
```

```python
import functools

import jax
import jax.numpy as jnp
from jax import lax
from jax.experimental import pallas as pl
from jax.experimental.pallas import tpu as pltpu
from jax.sharding import PartitionSpec as P

BF16 = jnp.bfloat16
F32 = jnp.float32
I32 = jnp.int32
SLOTS = 8
STEP = 16
WAYS = 4
LONG = 8
PIECES = 8
VMEM = pl.BlockSpec(memory_space=pltpu.VMEM)
HBM = pl.BlockSpec(memory_space=pltpu.HBM)
SMEM = pl.BlockSpec(memory_space=pltpu.SMEM)
NN = (((1,), (0,)), ((), ()))
NT = (((1,), (1,)), ((), ()))
TN = (((0,), (0,)), ((), ()))


def params(**kw):
    return pltpu.CompilerParams(vmem_limit_bytes=20 << 20, **kw)


def cost(flops, bytes_accessed):
    return pl.CostEstimate(flops=flops, bytes_accessed=bytes_accessed, transcendentals=0)


def send_out(buf, out_hbm, sems, piece):
    size = buf.shape[0] // sems.shape[0]
    at = pl.ds(piece * size, size)
    return pltpu.make_async_copy(buf.at[at], out_hbm.at[at], sems.at[piece])


def over_cols(value, here):
    groups = value.shape[0]
    rings = groups // 2
    value = value.reshape(rings, 2, *value.shape[1:])
    core, ring = here % 2, here // 2
    kept = lax.dynamic_index_in_dim(value, core, 1, keepdims=False)
    passed = lax.dynamic_index_in_dim(value, 1 - core, 1, keepdims=False)
    passed = lax.ppermute(passed, "cols", [(i, i ^ 1) for i in range(groups)])
    both = jnp.stack([kept, passed], axis=1)
    parts = []
    for far in range(rings):
        part = lax.dynamic_index_in_dim(both, (ring + far) % rings, 0, keepdims=False)
        if far:
            pairs = [(i, (i + 2 * far) % groups) for i in range(groups)]
            part = lax.ppermute(part, "cols", pairs)
        parts.append(part)
    return jnp.stack(parts)


def along(value, steps, peers):
    if not steps:
        return value
    pairs = [(i, i // LONG * LONG + (i + steps) % LONG) for i in range(peers)]
    return lax.ppermute(value, "rows", pairs)


def in_hbm(x):
    return pltpu.with_memory_space_constraint(x, pltpu.HBM)


def dot(a, b, dims):
    return lax.dot_general(a, b, dims, preferred_element_type=F32)


def position(col):
    return ((col >> 8) * 2 + ((col >> 5) & 1)) * (LONG // 2) + ((col >> 6) & 3)


def ranks(col, peers):
    peer, block = position(col), col & 31
    of_peer = (lax.broadcasted_iota(I32, (peers, col.shape[1]), 0) == peer).astype(F32)
    of_block = (lax.broadcasted_iota(I32, (32, col.shape[1]), 0) == block).astype(F32)
    counts = dot(of_peer.astype(BF16), of_block.astype(BF16), NT)
    present = (counts > 0.5).astype(F32)
    before = lower(32).astype(F32)
    return of_peer, of_block, present, dot(present.astype(BF16), before.astype(BF16), NN)


def lower(n):
    return lax.broadcasted_iota(I32, (n, n), 0) < lax.broadcasted_iota(I32, (n, n), 1)


def want_kernel(col_hbm, want_ref, col_buf, sem):
    copy = pltpu.make_async_copy(col_hbm, col_buf, sem)
    copy.start()
    copy.wait()
    relays, turns, _ = want_ref.shape
    peers = relays * turns
    _, _, present, rank = ranks(col_buf[...], peers)
    number = lax.broadcasted_iota(I32, (peers, 32), 1).astype(F32)
    lane = lax.broadcasted_iota(I32, (peers, 128), 1)
    want = jnp.zeros((peers, 128), F32)
    for s in range(SLOTS):
        chosen = jnp.sum(
            jnp.where(rank == float(s), present * number, 0.0), axis=1, keepdims=True
        )
        want = jnp.where(lane == s, chosen, want)
    want = want.astype(I32)
    for m in range(relays):
        want_ref[m] = want[m * turns : (m + 1) * turns, :]


def plan_kernel(peers, row_ref, col_ref, plan_ref):
    col, row = col_ref[...], row_ref[...]
    tiles = col.shape[1]
    of_peer, of_block, _, rank = ranks(col, peers)
    rank_of = dot(rank.astype(BF16), of_peer.astype(BF16), TN)
    tile_rank = jnp.sum(rank_of * of_block, axis=0, keepdims=True)
    own = ((col >> 5) == (row >> 5)).astype(F32)
    own_count = jnp.sum(own, axis=1, keepdims=True)
    earlier = lower(tiles).astype(F32).astype(BF16)
    far_peer = of_peer * (1.0 - own)
    same = dot(far_peer.astype(BF16), earlier, NN)
    totals = jnp.sum(far_peer, axis=1, keepdims=True)
    upper = (
        lax.broadcasted_iota(I32, (peers, peers), 0) > lax.broadcasted_iota(I32, (peers, peers), 1)
    ).astype(F32)
    wide = jnp.broadcast_to(totals, (peers, tiles))
    starts = dot(upper.astype(BF16), wide.astype(BF16), NN)
    ahead = jnp.sum(far_peer * (same + starts), axis=0, keepdims=True)
    own_ahead = dot(jnp.broadcast_to(own, (8, tiles)).astype(BF16), earlier, NN)[0:1]
    spot = jnp.where(own > 0.5, own_ahead, own_count + ahead)
    moved = (lax.broadcasted_iota(I32, (tiles, tiles), 0).astype(F32) == spot).astype(F32)
    values = jnp.concatenate(
        [
            lax.broadcasted_iota(I32, (1, tiles), 1).astype(F32),
            jnp.where(own > 0.5, float(peers), position(col).astype(F32)),
            jnp.where(own > 0.5, (col & 31).astype(F32), tile_rank),
            (row & 31).astype(F32),
            jnp.zeros((4, tiles), F32),
        ],
        axis=0,
    )
    ordered = dot(values.astype(BF16), moved.astype(BF16), NT)
    lanes = lax.broadcasted_iota(I32, (peers, tiles), 1)
    diagonal = (lanes == lax.broadcasted_iota(I32, (peers, tiles), 0)).astype(F32)
    firsts = own_count + jnp.sum(starts * diagonal, axis=0, keepdims=True)
    plan = jnp.concatenate(
        [
            ordered[0:1],
            ordered[1:2] * float(SLOTS) + ordered[2:3],
            ordered[3:4],
            jnp.broadcast_to(own_count, (1, tiles)),
            firsts,
            jnp.zeros((3, tiles), F32),
        ],
        axis=0,
    )
    plan_ref[...] = plan.astype(I32)


def pick_lanes(blocked, pick, high):
    width = 16
    spread = dot(blocked, pick, NN)
    total = jnp.zeros((width, pick.shape[1]), F32)
    for s in range(blocked.shape[0] // width):
        total = total + jnp.where(high == s, spread[s * width : (s + 1) * width], 0.0)
    return total.astype(BF16)


def permute_kernel(features_ref, order_ref, out_ref, blocked):
    count = order_ref.shape[0]
    width = features_ref.shape[0]
    for s in range(count):
        blocked[s * width : (s + 1) * width, :] = features_ref[:, s * 128 : (s + 1) * 128]
    low = lax.broadcasted_iota(I32, (128, 256), 0)
    for j in range(0, count, 2):
        o = jnp.concatenate([order_ref[j : j + 1, :], order_ref[j + 1 : j + 2, :]], axis=1)
        o = o & (count * 128 - 1)
        pick = jnp.where(low == (o & 127), 1.0, 0.0).astype(BF16)
        total = pick_lanes(blocked[...], pick, o >> 7)
        out_ref[j] = total[:, :128]
        out_ref[j + 1] = total[:, 128:]


def pack_kernel(here_ref, asked_ref, *refs):
    held, (send_hbm, buf, sems) = refs[:-3], refs[-3:]
    pieces = sems.shape[0]
    members = buf.shape[0] // pieces
    for piece in range(pieces):
        for m in range(piece * members, (piece + 1) * members):
            for far, blocks_ref in enumerate(held):
                k = (here_ref[0] + far) % len(held)
                for s in range(SLOTS):
                    buf[m, k * SLOTS + s] = blocks_ref[asked_ref[m, k, s]]
        send_out(buf, send_hbm, sems, piece).start()
    for piece in range(pieces):
        send_out(buf, send_hbm, sems, piece).wait()


def chunk_copy(tiles_hbm, tiles, sems, i):
    at = pl.ds(i * STEP, STEP)
    return pltpu.make_async_copy(tiles_hbm.at[at], tiles.at[at], sems.at[i])


def fetch_tiles(first, last, tiles_hbm, tiles, sems):
    def start(i, carry):
        chunk_copy(tiles_hbm, tiles, sems, i).start()
        return carry

    lax.fori_loop(first, last, start, 0)


def add_products(plan_ref, first, last, left, tile, dims, into, spare, prod, total, arrive=None):
    def step(i, carry):
        if arrive is not None:
            arrive(i)
        for u in range(STEP):
            k = i * STEP + u
            prod[u] = dot(left(k), tile(k), dims)
        for u in range(STEP):
            k = i * STEP + u
            at = jnp.where((k >= first) & (k < last), into(k), spare)
            total[at] = total[at] + prod[u]
        return carry

    lax.fori_loop(first // STEP, (last + STEP - 1) // STEP, step, 0)


def forward_own_kernel(base, plan_ref, own_ref, tiles_hbm, out_ref, list_hbm, prod, total, tiles, sem, out_sem):
    count = own_ref.shape[0]
    for k in range(tiles.shape[0]):
        pltpu.make_async_copy(tiles_hbm.at[plan_ref[0, k]], tiles.at[k], sem).start()
    pltpu.make_async_copy(tiles_hbm, tiles, sem).wait()
    store = pltpu.make_async_copy(tiles, list_hbm, out_sem)
    store.start()
    total[...] = jnp.zeros_like(total)
    add_products(
        plan_ref,
        0,
        plan_ref[3, 0],
        lambda k: own_ref[jnp.maximum(plan_ref[1, k] - base, 0)],
        lambda k: tiles[k],
        NT,
        lambda k: plan_ref[2, k],
        count,
        prod,
        total,
    )
    out_ref[...] = total[:count]
    store.wait()


def forward_kernel(plan_ref, got_ref, part_ref, tiles_hbm, out_ref, prod, total, tiles, sems):
    first = plan_ref[3, 0]

    fetch_tiles(first // STEP, tiles.shape[0] // STEP, tiles_hbm, tiles, sems)
    groups, per = out_ref.shape[:2]
    count = part_ref.shape[0]
    slots = got_ref.shape[0]
    total[:count] = part_ref[...]
    add_products(
        plan_ref,
        first,
        tiles.shape[0],
        lambda k: got_ref[jnp.minimum(plan_ref[1, k], slots - 1)],
        lambda k: tiles[k],
        NT,
        lambda k: plan_ref[2, k],
        count,
        prod,
        total,
        lambda i: chunk_copy(tiles_hbm, tiles, sems, i).wait(),
    )
    for c in range(groups):
        for b in range(per):
            out_ref[c, b] = total[c * per + b].astype(BF16)


def source(here, far, core):
    rings = 4
    y, c = here // 2, here % 2
    return (y + rings - far) % rings * 2 + (c + core) % 2


def dense_kernel(here_ref, weight_ref, got_ref, grad_ref, out_ref, act_hbm, grads, act_ref, sems):
    groups, per, width, _ = got_ref.shape
    for far in range(groups // 2):
        for core in range(2):
            grads[source(here_ref[0], far, core)] = grad_ref[far, core]
    inputs = groups * width
    weight = weight_ref[...]
    weight_t = weight.astype(F32).T.astype(BF16)
    part = jnp.zeros((inputs, inputs), F32)
    stores = []
    for b in range(per):
        agg = got_ref[:, b].reshape(inputs, 128)
        grad = grads[:, b].reshape(inputs, 128).astype(F32)
        pre = dot(weight_t, agg, NN)
        logistic = jax.nn.sigmoid(pre)
        act = (pre * logistic).astype(BF16)
        pre_grad = (grad * logistic * (1.0 + pre * (1.0 - logistic))).astype(BF16)
        agg_grad = dot(weight, pre_grad, NN).astype(BF16)
        part = part + dot(pre_grad, agg, NT)
        out_ref[:, b] = agg_grad.reshape(groups, width, 128)
        act_ref[:, b] = act.reshape(groups, width, 128)
        store = pltpu.make_async_copy(act_ref.at[:, b], act_hbm.at[:, b], sems.at[b])
        store.start()
        stores.append(store)
    high = part.astype(BF16)
    out_ref[:, per] = high.reshape(groups, width, 128)
    out_ref[:, per + 1] = (part - high.astype(F32)).astype(BF16).reshape(groups, width, 128)
    for store in stores:
        store.wait()


def backward_kernel(plan_ref, got_ref, tiles_hbm, send_hbm, prod, total, buf, sems, tiles, tile_sems):
    last = tiles.shape[0] // STEP
    begin = jnp.minimum(plan_ref[3, 0] // STEP, last - 1)

    fetch_tiles(begin, last, tiles_hbm, tiles, tile_sems)
    groups = got_ref.shape[0]
    per = got_ref.shape[1] - 2
    relays = buf.shape[0]
    each = buf.shape[1] - 1
    pieces = sems.shape[0]
    share = relays // pieces
    slots = relays * each
    total[...] = jnp.zeros_like(total)
    part = got_ref[0, per].astype(F32) + got_ref[0, per + 1].astype(F32)
    for c in range(1, groups):
        part = part + got_ref[c, per].astype(F32) + got_ref[c, per + 1].astype(F32)
    part = part.astype(BF16)
    for m in range(relays):
        buf[m, each] = part

    def step(i, carry):
        chunk_copy(tiles_hbm, tiles, tile_sems, i).wait()
        for u in range(STEP):
            r = plan_ref[2, i * STEP + u]
            prod[u] = dot(got_ref[r // per, r % per], tiles[i * STEP + u], NN)
        for u in range(STEP):
            k = i * STEP + u
            at = jnp.where(k >= plan_ref[3, 0], jnp.minimum(plan_ref[1, k], slots), slots)
            total[at] = total[at] + prod[u]
        done = (i + 1) * STEP
        for piece in range(pieces):
            until = plan_ref[4, (piece + 1) * share * each // SLOTS] if piece + 1 < pieces else last * STEP

            @pl.when((until <= done) & ((until > i * STEP) | (i == begin)))
            def _():
                for m in range(piece * share, (piece + 1) * share):
                    buf[m, :each] = total[m * each : (m + 1) * each].astype(BF16)
                send_out(buf, send_hbm, sems, piece).start()

        return carry

    lax.fori_loop(begin, last, step, 0)
    for piece in range(pieces):
        send_out(buf, send_hbm, sems, piece).wait()


def backward_own_kernel(
    base, plan_ref, got_ref, tiles_hbm, order_ref, out_hbm, inverse_ref, pick_ref, prod, total, tiles, sems, spots, low_pick, out_sem
):
    fetch_tiles(0, (plan_ref[3, 0] + STEP - 1) // STEP, tiles_hbm, tiles, sems)
    count, width = out_hbm.shape[:2]
    per = got_ref.shape[1] - 2
    total[...] = jnp.zeros_like(total)
    add_products(
        plan_ref,
        0,
        plan_ref[3, 0],
        lambda k: got_ref[plan_ref[2, k] // per, plan_ref[2, k] % per],
        lambda k: tiles[k],
        NN,
        lambda k: jnp.maximum(plan_ref[1, k] - base, 0),
        count,
        prod,
        total,
        lambda i: chunk_copy(tiles_hbm, tiles, sems, i).wait(),
    )
    store = pltpu.make_async_copy(total.at[pl.ds(0, count)], out_hbm, out_sem)
    store.start()
    low = lax.broadcasted_iota(I32, (128, 128), 0)
    source = lax.broadcasted_iota(I32, (count, 128), 0)
    lane = lax.broadcasted_iota(I32, (count, 128), 1).astype(F32)
    for j in range(count):
        o = order_ref[j : j + 1, :] & (count * 128 - 1)
        lanes = slice(j * 128, (j + 1) * 128)
        low_pick[:, lanes] = jnp.where(low == (o & 127), 1.0, 0.0).astype(BF16)
        here = source == (o >> 7)
        spots[:count, lanes] = jnp.where(here, float(j), 0.0).astype(BF16)
        spots[count:, lanes] = jnp.where(here, lane, 0.0).astype(BF16)
    inverse = dot(spots[...], low_pick[...], NT).astype(I32)
    odd = lax.broadcasted_iota(I32, (256, 128), 0)
    for j in range(count):
        at = inverse[count + j : count + j + 1, :] + (inverse[j : j + 1, :] & 1) * 128
        pick_ref[:, j * 128 : (j + 1) * 128] = jnp.where(odd == at, 1.0, 0.0).astype(BF16)
    inverse_ref[...] = inverse[:count] >> 1
    store.wait()


def blocks_kernel(grad_ref, out_ref):
    groups, per = out_ref.shape[:2]
    for c in range(groups):
        for b in range(per):
            at = (c * per + b) * 128
            out_ref[c, b] = grad_ref[:, at : at + 128]


def lanes_kernel(here_ref, got_ref, out_ref):
    for far in range(got_ref.shape[0]):
        for core in range(2):
            at = source(here_ref[0], far, core) * got_ref.shape[2]
            for b in range(got_ref.shape[2]):
                out_ref[:, pl.ds(pl.multiple_of((at + b) * 128, 128), 128)] = got_ref[far, core, b]


def relay_kernel(turn_ref, asked_ref, got_ref, own_ref, *refs):
    outs, totals = refs[: -WAYS], refs[-WAYS:]
    members, each = got_ref.shape[:2]
    each = each - 1
    turns = each // SLOTS
    count = own_ref.shape[0] - 1
    for total in totals:
        total[...] = jnp.zeros_like(total)
    for m in range(0, members, WAYS):
        for k in range(turns):
            for s in range(SLOTS):
                for w, total in enumerate(totals):
                    at = k * count + asked_ref[m + w, k, s]
                    total[at] = total[at] + got_ref[m + w, k * SLOTS + s].astype(F32)
    part = got_ref[0, each].astype(F32)
    for m in range(1, members):
        part = part + got_ref[m, each].astype(F32)
    own_ref[count] = part
    high = part.astype(BF16)
    low = (part - high.astype(F32)).astype(BF16)
    for far in range(turns):
        at = pl.ds((turn_ref[0] + far) % turns * count, count)
        value = totals[0][at]
        for total in totals[1:]:
            value = value + total[at]
        if far:
            outs[far - 1][:count] = value.astype(BF16)
            outs[far - 1][count] = high
            outs[far - 1][count + 1] = low
        else:
            own_ref[:count] = value


def final_kernel(scale, kept_hbm, own_ref, one_ref, two_ref, three_ref, inverse_ref, pick_ref, grads_ref, weight_ref, kept, sem):
    fetch = pltpu.make_async_copy(kept_hbm, kept, sem)
    fetch.start()
    count = kept.shape[0]
    part, node = own_ref[count], own_ref[:count]
    for ref in (one_ref, two_ref, three_ref):
        part = part + ref[count].astype(F32) + ref[count + 1].astype(F32)
        node = node + ref[:count].astype(F32)
    weight_ref[...] = part * scale
    fetch.wait()
    node = (node + kept[...]).astype(BF16)
    blocked = jnp.concatenate(
        [jnp.concatenate([node[j], node[j + 1]], axis=1) for j in range(0, count, 2)], axis=0
    )
    for j in range(0, count, 2):
        high = jnp.concatenate([inverse_ref[j : j + 1, :], inverse_ref[j + 1 : j + 2, :]], axis=1)
        lanes = slice(j * 128, (j + 2) * 128)
        grads_ref[:, lanes] = pick_lanes(blocked, pick_ref[:, lanes], high)


def shards(features, node_order, tile_row, tile_col, tile_vals, weight, grad_out):
    width, span = features.shape
    tiles, size, _ = tile_vals.shape
    count = span // size
    peers = lax.axis_size("rows")
    groups = lax.axis_size("cols")
    per = count // groups
    order = node_order.reshape(count, size)
    shape = jax.ShapeDtypeStruct
    prod = pltpu.VMEM((STEP, width, size), F32)
    tile_buf = pltpu.VMEM(tile_vals.shape, BF16)
    sums = lambda n: pltpu.VMEM((n + 1, width, size), F32)

    relays, turns = 2 * (peers // LONG), LONG // 2
    turn = lax.axis_index("rows") % LONG // 2
    turn_at = turn.reshape(1)
    near = [
        [x * LONG + 2 * j + q for x in range(peers // LONG) for q in range(2)] for j in range(turns)
    ]
    swap = lambda v: lax.all_to_all(v, "rows", 0, 0, tiled=True, axis_index_groups=near)

    with jax.named_scope("permute"):
        own = pl.pallas_call(
            permute_kernel,
            out_shape=shape((count, width, size), BF16),
            in_specs=[VMEM, VMEM],
            out_specs=VMEM,
            scratch_shapes=[pltpu.VMEM((count * width, size), BF16)],
            compiler_params=params(),
            cost_estimate=cost(1 << 31, 1 << 22),
        )(features, order)
        held = [own] + [along(own, -2 * far, peers) for far in range(1, turns)]

    with jax.named_scope("index"):
        rows, cols = tile_row.reshape(1, tiles), tile_col.reshape(1, tiles)
        want = pl.pallas_call(
            want_kernel,
            out_shape=shape((relays, turns, 128), I32),
            in_specs=[HBM],
            out_specs=VMEM,
            scratch_shapes=[pltpu.VMEM((1, tiles), I32), pltpu.SemaphoreType.DMA],
            compiler_params=params(),
        )(in_hbm(cols))
        asked = swap(want)
        plan = pl.pallas_call(
            functools.partial(plan_kernel, peers),
            out_shape=shape((8, tiles), I32),
            in_specs=[VMEM, VMEM],
            out_specs=VMEM,
            compiler_params=params(),
            cost_estimate=cost(1 << 30, 1 << 21),
        )(rows, cols)

    with jax.named_scope("pack"):
        send = pl.pallas_call(
            pack_kernel,
            out_shape=shape((relays, turns * SLOTS, width, size), BF16),
            in_specs=[SMEM, SMEM] + [VMEM] * turns,
            out_specs=HBM,
            scratch_shapes=[
                pltpu.VMEM((relays, turns * SLOTS, width, size), BF16),
                pltpu.SemaphoreType.DMA((min(PIECES, relays),)),
            ],
            compiler_params=params(),
        )(turn_at, asked, *held)
        got = swap(send)

    with jax.named_scope("forward_own"):
        part, tile_list = pl.pallas_call(
            functools.partial(forward_own_kernel, peers * SLOTS),
            out_shape=(shape((count, width, size), F32), pltpu.HBM(tile_vals.shape, BF16)),
            in_specs=[SMEM, VMEM, HBM],
            out_specs=(VMEM, HBM),
            scratch_shapes=[prod, sums(count), tile_buf, pltpu.SemaphoreType.DMA, pltpu.SemaphoreType.DMA],
            compiler_params=params(),
            cost_estimate=cost(1 << 31, 1 << 22),
        )(plan, own, in_hbm(tile_vals))

    with jax.named_scope("grads"):
        here = lax.axis_index("cols")
        grad_out, part = lax.optimization_barrier((grad_out, part))
        grads = pl.pallas_call(
            blocks_kernel,
            out_shape=shape((groups, per, width, size), BF16),
            in_specs=[VMEM],
            out_specs=VMEM,
            compiler_params=params(),
        )(grad_out)
        grads, part = lax.optimization_barrier((over_cols(grads, here), part))
        here_at = here.reshape(1)

    with jax.named_scope("forward"):
        mixed = pl.pallas_call(
            forward_kernel,
            out_shape=shape((groups, per, width, size), BF16),
            in_specs=[SMEM, VMEM, VMEM, HBM],
            out_specs=VMEM,
            scratch_shapes=[prod, sums(count), tile_buf, pltpu.SemaphoreType.DMA((tiles // STEP,))],
            compiler_params=params(),
            cost_estimate=cost(1 << 30, 1 << 22),
        )(plan, got.reshape(peers * SLOTS, width, size), part, in_hbm(tile_list))
        mixed = lax.all_to_all(mixed, "cols", 0, 0, tiled=True)

    with jax.named_scope("dense"):
        back, act = pl.pallas_call(
            dense_kernel,
            out_shape=(
                shape((groups, per + 2, width, size), BF16),
                pltpu.HBM((groups, per, width, size), BF16),
            ),
            in_specs=[SMEM, VMEM, VMEM, VMEM],
            out_specs=(VMEM, HBM),
            scratch_shapes=[pltpu.VMEM((groups, per, width, size), BF16)] * 2
            + [pltpu.SemaphoreType.DMA((per,))],
            compiler_params=params(),
        )(here_at, weight, mixed, grads)
        back = lax.all_to_all(back, "cols", 0, 0, tiled=True)

    with jax.named_scope("backward"):
        parts = pl.pallas_call(
            backward_kernel,
            out_shape=shape((relays, turns * SLOTS + 1, width, size), BF16),
            in_specs=[SMEM, VMEM, HBM],
            out_specs=HBM,
            scratch_shapes=[
                prod,
                sums(peers * SLOTS),
                pltpu.VMEM((relays, turns * SLOTS + 1, width, size), BF16),
                pltpu.SemaphoreType.DMA((4,)),
                tile_buf,
                pltpu.SemaphoreType.DMA((tiles // STEP,)),
            ],
            compiler_params=params(),
            cost_estimate=cost(1 << 30, 1 << 22),
        )(plan, back, in_hbm(tile_list))
        parts = swap(parts)

    with jax.named_scope("backward_own"):
        kept, inverse, pick = pl.pallas_call(
            functools.partial(backward_own_kernel, peers * SLOTS),
            out_shape=(
                pltpu.HBM((count, width, size), F32),
                shape((count, size), I32),
                shape((2 * size, span), BF16),
            ),
            in_specs=[SMEM, VMEM, HBM, VMEM],
            out_specs=(HBM, VMEM, VMEM),
            scratch_shapes=[
                prod,
                sums(count),
                tile_buf,
                pltpu.SemaphoreType.DMA((tiles // STEP,)),
                pltpu.VMEM((2 * count, span), BF16),
                pltpu.VMEM((size, span), BF16),
                pltpu.SemaphoreType.DMA,
            ],
            compiler_params=params(),
            cost_estimate=cost(1 << 31, 1 << 22),
        )(plan, back, in_hbm(tile_list), order)

    with jax.named_scope("activated"):
        act, kept = lax.optimization_barrier((act, kept))
        activated = pl.pallas_call(
            lanes_kernel,
            out_shape=shape((width, span), BF16),
            in_specs=[SMEM, VMEM],
            out_specs=VMEM,
            compiler_params=params(),
        )(here_at, over_cols(act, here))

    with jax.named_scope("relay"):
        sums_of = pl.pallas_call(
            relay_kernel,
            out_shape=(shape((count + 1, width, size), F32),)
            + (shape((count + 2, width, size), BF16),) * (turns - 1),
            in_specs=[SMEM, SMEM, VMEM],
            out_specs=(VMEM,) * turns,
            scratch_shapes=[pltpu.VMEM((turns * count, width, size), F32)] * WAYS,
            compiler_params=params(),
        )(turn_at, asked, parts)
        sums_of = [along(v, 2 * far, peers) for far, v in enumerate(sums_of)]

    with jax.named_scope("final"):
        feat_grads, weight_grad = pl.pallas_call(
            functools.partial(final_kernel, float(peers * span) ** -0.5),
            out_shape=(shape((width, span), BF16), shape((width, size), F32)),
            in_specs=[HBM] + [VMEM] * (turns + 2),
            out_specs=(VMEM, VMEM),
            scratch_shapes=[pltpu.VMEM((count, width, size), F32), pltpu.SemaphoreType.DMA],
            compiler_params=params(),
        )(in_hbm(kept), *sums_of, inverse, pick)
    return activated, feat_grads, weight_grad.T


def solution(mesh):
    in_specs = (
        P("cols", "rows"),
        P("rows"),
        P("rows"),
        P("rows"),
        P("rows", None, None),
        P(),
        P("cols", "rows"),
    )
    out_specs = (P("cols", "rows"), P("cols", "rows"), P(None, "cols"))
    return jax.shard_map(shards, mesh=mesh, in_specs=in_specs, out_specs=out_specs, check_vma=False)
```

```python
import functools

import jax
import jax.numpy as jnp
from jax import lax
from jax.experimental import pallas as pl
from jax.experimental.pallas import tpu as pltpu
from jax.sharding import PartitionSpec as P

BF16 = jnp.bfloat16
F32 = jnp.float32
I32 = jnp.int32
SLOTS = 8
STEP = 16
WAYS = 4
LONG = 8
PIECES = 8
VMEM = pl.BlockSpec(memory_space=pltpu.VMEM)
HBM = pl.BlockSpec(memory_space=pltpu.HBM)
SMEM = pl.BlockSpec(memory_space=pltpu.SMEM)
NN = (((1,), (0,)), ((), ()))
NT = (((1,), (1,)), ((), ()))
TN = (((0,), (0,)), ((), ()))


def params(**kw):
    return pltpu.CompilerParams(vmem_limit_bytes=20 << 20, **kw)


def cost(flops, bytes_accessed):
    return pl.CostEstimate(flops=flops, bytes_accessed=bytes_accessed, transcendentals=0)


def send_out(buf, out_hbm, sems, piece):
    size = buf.shape[0] // sems.shape[0]
    at = pl.ds(piece * size, size)
    return pltpu.make_async_copy(buf.at[at], out_hbm.at[at], sems.at[piece])


def over_cols(value, here):
    groups = value.shape[0]
    rings = groups // 2
    value = value.reshape(rings, 2, *value.shape[1:])
    core, ring = here % 2, here // 2
    kept = lax.dynamic_index_in_dim(value, core, 1, keepdims=False)
    passed = lax.dynamic_index_in_dim(value, 1 - core, 1, keepdims=False)
    passed = lax.ppermute(passed, "cols", [(i, i ^ 1) for i in range(groups)])
    both = jnp.stack([kept, passed], axis=1)
    parts = []
    for far in range(rings):
        part = lax.dynamic_index_in_dim(both, (ring + far) % rings, 0, keepdims=False)
        if far:
            pairs = [(i, (i + 2 * far) % groups) for i in range(groups)]
            part = lax.ppermute(part, "cols", pairs)
        parts.append(part)
    return jnp.stack(parts)


def along(value, steps, peers):
    if not steps:
        return value
    pairs = [(i, i // LONG * LONG + (i + steps) % LONG) for i in range(peers)]
    return lax.ppermute(value, "rows", pairs)


def in_hbm(x):
    return pltpu.with_memory_space_constraint(x, pltpu.HBM)


def dot(a, b, dims):
    return lax.dot_general(a, b, dims, preferred_element_type=F32)


def position(col):
    return ((col >> 8) * 2 + ((col >> 5) & 1)) * (LONG // 2) + ((col >> 6) & 3)


def ranks(col, peers):
    peer, block = position(col), col & 31
    of_peer = (lax.broadcasted_iota(I32, (peers, col.shape[1]), 0) == peer).astype(F32)
    of_block = (lax.broadcasted_iota(I32, (32, col.shape[1]), 0) == block).astype(F32)
    counts = dot(of_peer.astype(BF16), of_block.astype(BF16), NT)
    present = (counts > 0.5).astype(F32)
    before = lower(32).astype(F32)
    return of_peer, of_block, present, dot(present.astype(BF16), before.astype(BF16), NN)


def lower(n):
    return lax.broadcasted_iota(I32, (n, n), 0) < lax.broadcasted_iota(I32, (n, n), 1)


def start_kernel(
    row_hbm,
    col_hbm,
    features_hbm,
    order_hbm,
    want_hbm,
    out_ref,
    plan_ref,
    row_ref,
    col_ref,
    features_ref,
    order_ref,
    want_ref,
    blocked,
    sems,
):
    copies = [
        pltpu.make_async_copy(col_hbm, col_ref, sems.at[0]),
        pltpu.make_async_copy(features_hbm, features_ref, sems.at[1]),
        pltpu.make_async_copy(order_hbm, order_ref, sems.at[2]),
        pltpu.make_async_copy(row_hbm, row_ref, sems.at[4]),
    ]
    for copy in copies:
        copy.start()
    copies[0].wait()
    relays, turns, _ = want_ref.shape
    peers = relays * turns
    of_peer, of_block, present, rank = ranks(col_ref[...], peers)
    number = lax.broadcasted_iota(I32, (peers, 32), 1).astype(F32)
    lane = lax.broadcasted_iota(I32, (peers, 128), 1)
    want = jnp.zeros((peers, 128), F32)
    for s in range(SLOTS):
        chosen = jnp.sum(
            jnp.where(rank == float(s), present * number, 0.0), axis=1, keepdims=True
        )
        want = jnp.where(lane == s, chosen, want)
    want = want.astype(I32)
    for m in range(relays):
        want_ref[m] = want[m * turns : (m + 1) * turns, :]
    store = pltpu.make_async_copy(want_ref, want_hbm, sems.at[3])
    store.start()
    for copy in copies[1:]:
        copy.wait()
    plan_ref[...] = lay_out(peers, row_ref[...], col_ref[...], of_peer, of_block, rank)
    permute(features_ref, order_ref, out_ref, blocked)
    store.wait()


def lay_out(peers, row, col, of_peer, of_block, rank):
    tiles = col.shape[1]
    rank_of = dot(rank.astype(BF16), of_peer.astype(BF16), TN)
    tile_rank = jnp.sum(rank_of * of_block, axis=0, keepdims=True)
    own = ((col >> 5) == (row >> 5)).astype(F32)
    own_count = jnp.sum(own, axis=1, keepdims=True)
    earlier = lower(tiles).astype(F32).astype(BF16)
    far_peer = of_peer * (1.0 - own)
    same = dot(far_peer.astype(BF16), earlier, NN)
    totals = jnp.sum(far_peer, axis=1, keepdims=True)
    upper = (
        lax.broadcasted_iota(I32, (peers, peers), 0) > lax.broadcasted_iota(I32, (peers, peers), 1)
    ).astype(F32)
    wide = jnp.broadcast_to(totals, (peers, tiles))
    starts = dot(upper.astype(BF16), wide.astype(BF16), NN)
    ahead = jnp.sum(far_peer * (same + starts), axis=0, keepdims=True)
    own_ahead = dot(jnp.broadcast_to(own, (8, tiles)).astype(BF16), earlier, NN)[0:1]
    spot = jnp.where(own > 0.5, own_ahead, own_count + ahead)
    moved = (lax.broadcasted_iota(I32, (tiles, tiles), 0).astype(F32) == spot).astype(F32)
    values = jnp.concatenate(
        [
            lax.broadcasted_iota(I32, (1, tiles), 1).astype(F32),
            jnp.where(own > 0.5, float(peers), position(col).astype(F32)),
            jnp.where(own > 0.5, (col & 31).astype(F32), tile_rank),
            (row & 31).astype(F32),
            jnp.zeros((4, tiles), F32),
        ],
        axis=0,
    )
    ordered = dot(values.astype(BF16), moved.astype(BF16), NT)
    lanes = lax.broadcasted_iota(I32, (peers, tiles), 1)
    diagonal = (lanes == lax.broadcasted_iota(I32, (peers, tiles), 0)).astype(F32)
    firsts = own_count + jnp.sum(starts * diagonal, axis=0, keepdims=True)
    plan = jnp.concatenate(
        [
            ordered[0:1],
            ordered[1:2] * float(SLOTS) + ordered[2:3],
            ordered[3:4],
            jnp.broadcast_to(own_count, (1, tiles)),
            firsts,
            jnp.zeros((3, tiles), F32),
        ],
        axis=0,
    )
    return plan.astype(I32)


def pick_lanes(blocked, pick, high):
    width = 16
    spread = dot(blocked, pick, NN)
    total = jnp.zeros((width, pick.shape[1]), F32)
    for s in range(blocked.shape[0] // width):
        total = total + jnp.where(high == s, spread[s * width : (s + 1) * width], 0.0)
    return total.astype(BF16)


def permute(features_ref, order_ref, out_ref, blocked):
    count = order_ref.shape[0]
    width = features_ref.shape[0]
    for s in range(count):
        blocked[s * width : (s + 1) * width, :] = features_ref[:, s * 128 : (s + 1) * 128]
    low = lax.broadcasted_iota(I32, (128, 256), 0)
    for j in range(0, count, 2):
        o = jnp.concatenate([order_ref[j : j + 1, :], order_ref[j + 1 : j + 2, :]], axis=1)
        o = o & (count * 128 - 1)
        pick = jnp.where(low == (o & 127), 1.0, 0.0).astype(BF16)
        total = pick_lanes(blocked[...], pick, o >> 7)
        out_ref[j] = total[:, :128]
        out_ref[j + 1] = total[:, 128:]


def pack_kernel(here_ref, asked_ref, *refs):
    held, (send_hbm, buf, sems) = refs[:-3], refs[-3:]
    pieces = sems.shape[0]
    members = buf.shape[0] // pieces
    for piece in range(pieces):
        for m in range(piece * members, (piece + 1) * members):
            for far, blocks_ref in enumerate(held):
                k = (here_ref[0] + far) % len(held)
                for s in range(SLOTS):
                    buf[m, k * SLOTS + s] = blocks_ref[asked_ref[m, k, s]]
        send_out(buf, send_hbm, sems, piece).start()
    for piece in range(pieces):
        send_out(buf, send_hbm, sems, piece).wait()


def chunk_copy(tiles_hbm, tiles, sems, i):
    at = pl.ds(i * STEP, STEP)
    return pltpu.make_async_copy(tiles_hbm.at[at], tiles.at[at], sems.at[i])


def fetch_tiles(first, last, tiles_hbm, tiles, sems):
    def start(i, carry):
        chunk_copy(tiles_hbm, tiles, sems, i).start()
        return carry

    lax.fori_loop(first, last, start, 0)


def add_products(plan_ref, first, last, left, tile, dims, into, spare, prod, total, arrive=None):
    def step(i, carry):
        if arrive is not None:
            arrive(i)
        for u in range(STEP):
            k = i * STEP + u
            prod[u] = dot(left(k), tile(k), dims)
        for u in range(STEP):
            k = i * STEP + u
            at = jnp.where((k >= first) & (k < last), into(k), spare)
            total[at] = total[at] + prod[u]
        return carry

    lax.fori_loop(first // STEP, (last + STEP - 1) // STEP, step, 0)


def forward_own_kernel(base, plan_ref, own_ref, tiles_hbm, out_ref, list_hbm, prod, total, tiles, sem, out_sem):
    count = own_ref.shape[0]
    for k in range(tiles.shape[0]):
        pltpu.make_async_copy(tiles_hbm.at[plan_ref[0, k]], tiles.at[k], sem).start()
    pltpu.make_async_copy(tiles_hbm, tiles, sem).wait()
    store = pltpu.make_async_copy(tiles, list_hbm, out_sem)
    store.start()
    total[...] = jnp.zeros_like(total)
    add_products(
        plan_ref,
        0,
        plan_ref[3, 0],
        lambda k: own_ref[jnp.maximum(plan_ref[1, k] - base, 0)],
        lambda k: tiles[k],
        NT,
        lambda k: plan_ref[2, k],
        count,
        prod,
        total,
    )
    out_ref[...] = total[:count]
    store.wait()


def forward_kernel(plan_ref, got_ref, part_ref, tiles_hbm, out_ref, prod, total, tiles, sems):
    first = plan_ref[3, 0]

    fetch_tiles(first // STEP, tiles.shape[0] // STEP, tiles_hbm, tiles, sems)
    groups, per = out_ref.shape[:2]
    count = part_ref.shape[0]
    slots = got_ref.shape[0]
    total[:count] = part_ref[...]
    add_products(
        plan_ref,
        first,
        tiles.shape[0],
        lambda k: got_ref[jnp.minimum(plan_ref[1, k], slots - 1)],
        lambda k: tiles[k],
        NT,
        lambda k: plan_ref[2, k],
        count,
        prod,
        total,
        lambda i: chunk_copy(tiles_hbm, tiles, sems, i).wait(),
    )
    for c in range(groups):
        for b in range(per):
            out_ref[c, b] = total[c * per + b].astype(BF16)


def source(here, far, core):
    rings = 4
    y, c = here // 2, here % 2
    return (y + rings - far) % rings * 2 + (c + core) % 2


def dense_kernel(here_ref, weight_ref, got_ref, grad_ref, out_ref, act_hbm, grads, act_ref, sems):
    groups, per, width, _ = got_ref.shape
    for far in range(groups // 2):
        for core in range(2):
            grads[source(here_ref[0], far, core)] = grad_ref[far, core]
    inputs = groups * width
    weight = weight_ref[...]
    weight_t = weight.astype(F32).T.astype(BF16)
    part = jnp.zeros((inputs, inputs), F32)
    stores, pre_grads = [], []
    for b in range(per):
        agg = got_ref[:, b].reshape(inputs, 128)
        grad = grads[:, b].reshape(inputs, 128).astype(F32)
        pre = dot(weight_t, agg, NN)
        logistic = jax.nn.sigmoid(pre)
        act = (pre * logistic).astype(BF16)
        pre_grad = (grad * logistic * (1.0 + pre * (1.0 - logistic))).astype(BF16)
        pre_grads.append(pre_grad)
        act_ref[:, b] = act.reshape(groups, width, 128)
        store = pltpu.make_async_copy(act_ref.at[:, b], act_hbm.at[:, b], sems.at[b])
        store.start()
        stores.append(store)
    for b, pre_grad in enumerate(pre_grads):
        agg_grad = dot(weight, pre_grad, NN).astype(BF16)
        part = part + dot(pre_grad, got_ref[:, b].reshape(inputs, 128), NT)
        out_ref[:, b] = agg_grad.reshape(groups, width, 128)
    high = part.astype(BF16)
    out_ref[:, per] = high.reshape(groups, width, 128)
    out_ref[:, per + 1] = (part - high.astype(F32)).astype(BF16).reshape(groups, width, 128)
    for store in stores:
        store.wait()


def backward_kernel(plan_ref, got_ref, tiles_hbm, send_hbm, prod, total, buf, sems, tiles, tile_sems):
    last = tiles.shape[0] // STEP
    begin = jnp.minimum(plan_ref[3, 0] // STEP, last - 1)

    fetch_tiles(begin, last, tiles_hbm, tiles, tile_sems)
    groups = got_ref.shape[0]
    per = got_ref.shape[1] - 2
    relays = buf.shape[0]
    each = buf.shape[1] - 1
    pieces = sems.shape[0]
    share = relays // pieces
    slots = relays * each
    total[...] = jnp.zeros_like(total)
    part = got_ref[0, per].astype(F32) + got_ref[0, per + 1].astype(F32)
    for c in range(1, groups):
        part = part + got_ref[c, per].astype(F32) + got_ref[c, per + 1].astype(F32)
    part = part.astype(BF16)
    for m in range(relays):
        buf[m, each] = part

    def step(i, carry):
        chunk_copy(tiles_hbm, tiles, tile_sems, i).wait()
        for u in range(STEP):
            r = plan_ref[2, i * STEP + u]
            prod[u] = dot(got_ref[r // per, r % per], tiles[i * STEP + u], NN)
        for u in range(STEP):
            k = i * STEP + u
            at = jnp.where(k >= plan_ref[3, 0], jnp.minimum(plan_ref[1, k], slots), slots)
            total[at] = total[at] + prod[u]
        done = (i + 1) * STEP
        for piece in range(pieces):
            until = plan_ref[4, (piece + 1) * share * each // SLOTS] if piece + 1 < pieces else last * STEP

            @pl.when((until <= done) & ((until > i * STEP) | (i == begin)))
            def _():
                for m in range(piece * share, (piece + 1) * share):
                    buf[m, :each] = total[m * each : (m + 1) * each].astype(BF16)
                send_out(buf, send_hbm, sems, piece).start()

        return carry

    lax.fori_loop(begin, last, step, 0)
    for piece in range(pieces):
        send_out(buf, send_hbm, sems, piece).wait()


def backward_own_kernel(
    base, plan_ref, got_ref, tiles_hbm, order_ref, out_hbm, inverse_ref, pick_ref, prod, total, tiles, sems, spots, low_pick, out_sem
):
    fetch_tiles(0, (plan_ref[3, 0] + STEP - 1) // STEP, tiles_hbm, tiles, sems)
    count, width = out_hbm.shape[:2]
    per = got_ref.shape[1] - 2
    total[...] = jnp.zeros_like(total)
    add_products(
        plan_ref,
        0,
        plan_ref[3, 0],
        lambda k: got_ref[plan_ref[2, k] // per, plan_ref[2, k] % per],
        lambda k: tiles[k],
        NN,
        lambda k: jnp.maximum(plan_ref[1, k] - base, 0),
        count,
        prod,
        total,
        lambda i: chunk_copy(tiles_hbm, tiles, sems, i).wait(),
    )
    store = pltpu.make_async_copy(total.at[pl.ds(0, count)], out_hbm, out_sem)
    store.start()
    low = lax.broadcasted_iota(I32, (128, 128), 0)
    source = lax.broadcasted_iota(I32, (count, 128), 0)
    lane = lax.broadcasted_iota(I32, (count, 128), 1).astype(F32)
    for j in range(count):
        o = order_ref[j : j + 1, :] & (count * 128 - 1)
        lanes = slice(j * 128, (j + 1) * 128)
        low_pick[:, lanes] = jnp.where(low == (o & 127), 1.0, 0.0).astype(BF16)
        here = source == (o >> 7)
        spots[:count, lanes] = jnp.where(here, float(j), 0.0).astype(BF16)
        spots[count:, lanes] = jnp.where(here, lane, 0.0).astype(BF16)
    inverse = dot(spots[...], low_pick[...], NT).astype(I32)
    odd = lax.broadcasted_iota(I32, (256, 128), 0)
    for j in range(count):
        at = inverse[count + j : count + j + 1, :] + (inverse[j : j + 1, :] & 1) * 128
        pick_ref[:, j * 128 : (j + 1) * 128] = jnp.where(odd == at, 1.0, 0.0).astype(BF16)
    inverse_ref[...] = inverse[:count] >> 1
    store.wait()


def blocks_kernel(grad_ref, out_ref):
    groups, per = out_ref.shape[:2]
    for c in range(groups):
        for b in range(per):
            at = (c * per + b) * 128
            out_ref[c, b] = grad_ref[:, at : at + 128]


def lanes_kernel(here_ref, got_ref, out_ref):
    for far in range(got_ref.shape[0]):
        for core in range(2):
            at = source(here_ref[0], far, core) * got_ref.shape[2]
            for b in range(got_ref.shape[2]):
                out_ref[:, pl.ds(pl.multiple_of((at + b) * 128, 128), 128)] = got_ref[far, core, b]


def relay_kernel(turn_ref, asked_ref, got_ref, own_ref, *refs):
    outs, totals = refs[: -WAYS], refs[-WAYS:]
    members, each = got_ref.shape[:2]
    each = each - 1
    turns = each // SLOTS
    count = own_ref.shape[0] - 1
    for total in totals:
        total[...] = jnp.zeros_like(total)
    for m in range(0, members, WAYS):
        for k in range(turns):
            for s in range(SLOTS):
                for w, total in enumerate(totals):
                    at = k * count + asked_ref[m + w, k, s]
                    total[at] = total[at] + got_ref[m + w, k * SLOTS + s].astype(F32)
    part = got_ref[0, each].astype(F32)
    for m in range(1, members):
        part = part + got_ref[m, each].astype(F32)
    own_ref[count] = part
    high = part.astype(BF16)
    low = (part - high.astype(F32)).astype(BF16)
    for far in range(turns):
        at = pl.ds((turn_ref[0] + far) % turns * count, count)
        value = totals[0][at]
        for total in totals[1:]:
            value = value + total[at]
        if far:
            outs[far - 1][:count] = value.astype(BF16)
            outs[far - 1][count] = high
            outs[far - 1][count + 1] = low
        else:
            own_ref[:count] = value


def final_kernel(scale, kept_hbm, own_ref, one_ref, two_ref, three_ref, inverse_ref, pick_ref, grads_ref, weight_ref, kept, sem):
    fetch = pltpu.make_async_copy(kept_hbm, kept, sem)
    fetch.start()
    count = kept.shape[0]
    part, node = own_ref[count], own_ref[:count]
    for ref in (one_ref, two_ref, three_ref):
        part = part + ref[count].astype(F32) + ref[count + 1].astype(F32)
        node = node + ref[:count].astype(F32)
    weight_ref[...] = part * scale
    fetch.wait()
    node = (node + kept[...]).astype(BF16)
    blocked = jnp.concatenate(
        [jnp.concatenate([node[j], node[j + 1]], axis=1) for j in range(0, count, 2)], axis=0
    )
    for j in range(0, count, 2):
        high = jnp.concatenate([inverse_ref[j : j + 1, :], inverse_ref[j + 1 : j + 2, :]], axis=1)
        lanes = slice(j * 128, (j + 2) * 128)
        grads_ref[:, lanes] = pick_lanes(blocked, pick_ref[:, lanes], high)


def shards(features, node_order, tile_row, tile_col, tile_vals, weight, grad_out):
    width, span = features.shape
    tiles, size, _ = tile_vals.shape
    count = span // size
    peers = lax.axis_size("rows")
    groups = lax.axis_size("cols")
    per = count // groups
    order = node_order.reshape(count, size)
    shape = jax.ShapeDtypeStruct
    prod = pltpu.VMEM((STEP, width, size), F32)
    tile_buf = pltpu.VMEM(tile_vals.shape, BF16)
    sums = lambda n: pltpu.VMEM((n + 1, width, size), F32)

    relays, turns = 2 * (peers // LONG), LONG // 2
    turn = lax.axis_index("rows") % LONG // 2
    turn_at = turn.reshape(1)
    near = [
        [x * LONG + 2 * j + q for x in range(peers // LONG) for q in range(2)] for j in range(turns)
    ]
    swap = lambda v: lax.all_to_all(v, "rows", 0, 0, tiled=True, axis_index_groups=near)

    with jax.named_scope("start"):
        rows, cols = tile_row.reshape(1, tiles), tile_col.reshape(1, tiles)
        want, own, plan = pl.pallas_call(
            start_kernel,
            out_shape=(
                pltpu.HBM((relays, turns, 128), I32),
                shape((count, width, size), BF16),
                shape((8, tiles), I32),
            ),
            in_specs=[HBM] * 4,
            out_specs=(HBM, VMEM, VMEM),
            scratch_shapes=[
                pltpu.VMEM((1, tiles), I32),
                pltpu.VMEM((1, tiles), I32),
                pltpu.VMEM((width, span), BF16),
                pltpu.VMEM((count, size), I32),
                pltpu.VMEM((relays, turns, 128), I32),
                pltpu.VMEM((count * width, size), BF16),
                pltpu.SemaphoreType.DMA((5,)),
            ],
            compiler_params=params(),
        )(in_hbm(rows), in_hbm(cols), in_hbm(features), in_hbm(order))
        held = [own] + [along(own, -2 * far, peers) for far in (2, 1, 3)]
        held = [held[0], held[2], held[1], held[3]]
        asked = swap(want)

    with jax.named_scope("pack"):
        send = pl.pallas_call(
            pack_kernel,
            out_shape=shape((relays, turns * SLOTS, width, size), BF16),
            in_specs=[SMEM, SMEM] + [VMEM] * turns,
            out_specs=HBM,
            scratch_shapes=[
                pltpu.VMEM((relays, turns * SLOTS, width, size), BF16),
                pltpu.SemaphoreType.DMA((min(PIECES, relays),)),
            ],
            compiler_params=params(),
        )(turn_at, asked, *held)
    with jax.named_scope("grads"):
        here = lax.axis_index("cols")
        grad_out, send = lax.optimization_barrier((grad_out, send))
        got = swap(send)

    with jax.named_scope("forward_own"):
        part, tile_list = pl.pallas_call(
            functools.partial(forward_own_kernel, peers * SLOTS),
            out_shape=(shape((count, width, size), F32), pltpu.HBM(tile_vals.shape, BF16)),
            in_specs=[SMEM, VMEM, HBM],
            out_specs=(VMEM, HBM),
            scratch_shapes=[prod, sums(count), tile_buf, pltpu.SemaphoreType.DMA, pltpu.SemaphoreType.DMA],
            compiler_params=params(),
            cost_estimate=cost(1 << 31, 1 << 22),
        )(plan, own, in_hbm(tile_vals))

    with jax.named_scope("grads"):
        grads = pl.pallas_call(
            blocks_kernel,
            out_shape=shape((groups, per, width, size), BF16),
            in_specs=[VMEM],
            out_specs=VMEM,
            compiler_params=params(),
        )(grad_out)
        grads, part = lax.optimization_barrier((over_cols(grads, here), part))
        here_at = here.reshape(1)

    with jax.named_scope("forward"):
        mixed = pl.pallas_call(
            forward_kernel,
            out_shape=shape((groups, per, width, size), BF16),
            in_specs=[SMEM, VMEM, VMEM, HBM],
            out_specs=VMEM,
            scratch_shapes=[prod, sums(count), tile_buf, pltpu.SemaphoreType.DMA((tiles // STEP,))],
            compiler_params=params(),
            cost_estimate=cost(1 << 30, 1 << 22),
        )(plan, got.reshape(peers * SLOTS, width, size), part, in_hbm(tile_list))
        mixed = lax.all_to_all(mixed, "cols", 0, 0, tiled=True)

    with jax.named_scope("dense"):
        back, act = pl.pallas_call(
            dense_kernel,
            out_shape=(
                shape((groups, per + 2, width, size), BF16),
                pltpu.HBM((groups, per, width, size), BF16),
            ),
            in_specs=[SMEM, VMEM, VMEM, VMEM],
            out_specs=(VMEM, HBM),
            scratch_shapes=[pltpu.VMEM((groups, per, width, size), BF16)] * 2
            + [pltpu.SemaphoreType.DMA((per,))],
            compiler_params=params(),
        )(here_at, weight, mixed, grads)
        back = lax.all_to_all(back, "cols", 0, 0, tiled=True)

    with jax.named_scope("backward"):
        parts = pl.pallas_call(
            backward_kernel,
            out_shape=shape((relays, turns * SLOTS + 1, width, size), BF16),
            in_specs=[SMEM, VMEM, HBM],
            out_specs=HBM,
            scratch_shapes=[
                prod,
                sums(peers * SLOTS),
                pltpu.VMEM((relays, turns * SLOTS + 1, width, size), BF16),
                pltpu.SemaphoreType.DMA((4,)),
                tile_buf,
                pltpu.SemaphoreType.DMA((tiles // STEP,)),
            ],
            compiler_params=params(),
            cost_estimate=cost(1 << 30, 1 << 22),
        )(plan, back, in_hbm(tile_list))
        parts = swap(parts)

    with jax.named_scope("backward_own"):
        kept, inverse, pick = pl.pallas_call(
            functools.partial(backward_own_kernel, peers * SLOTS),
            out_shape=(
                pltpu.HBM((count, width, size), F32),
                shape((count, size), I32),
                shape((2 * size, span), BF16),
            ),
            in_specs=[SMEM, VMEM, HBM, VMEM],
            out_specs=(HBM, VMEM, VMEM),
            scratch_shapes=[
                prod,
                sums(count),
                tile_buf,
                pltpu.SemaphoreType.DMA((tiles // STEP,)),
                pltpu.VMEM((2 * count, span), BF16),
                pltpu.VMEM((size, span), BF16),
                pltpu.SemaphoreType.DMA,
            ],
            compiler_params=params(),
            cost_estimate=cost(1 << 31, 1 << 22),
        )(plan, back, in_hbm(tile_list), order)

    with jax.named_scope("activated"):
        act, kept = lax.optimization_barrier((act, kept))
        activated = pl.pallas_call(
            lanes_kernel,
            out_shape=shape((width, span), BF16),
            in_specs=[SMEM, VMEM],
            out_specs=VMEM,
            compiler_params=params(),
        )(here_at, over_cols(act, here))

    with jax.named_scope("relay"):
        sums_of = pl.pallas_call(
            relay_kernel,
            out_shape=(shape((count + 1, width, size), F32),)
            + (shape((count + 2, width, size), BF16),) * (turns - 1),
            in_specs=[SMEM, SMEM, VMEM],
            out_specs=(VMEM,) * turns,
            scratch_shapes=[pltpu.VMEM((turns * count, width, size), F32)] * WAYS,
            compiler_params=params(),
        )(turn_at, asked, parts)
        passed = {far: along(sums_of[far], 2 * far, peers) for far in (2, 1, 3)}
        sums_of = [sums_of[0]] + [passed[far] for far in (1, 2, 3)]

    with jax.named_scope("final"):
        feat_grads, weight_grad = pl.pallas_call(
            functools.partial(final_kernel, float(peers * span) ** -0.5),
            out_shape=(shape((width, span), BF16), shape((width, size), F32)),
            in_specs=[HBM] + [VMEM] * (turns + 2),
            out_specs=(VMEM, VMEM),
            scratch_shapes=[pltpu.VMEM((count, width, size), F32), pltpu.SemaphoreType.DMA],
            compiler_params=params(),
        )(in_hbm(kept), *sums_of, inverse, pick)
    return activated, feat_grads, weight_grad.T


def solution(mesh):
    in_specs = (
        P("cols", "rows"),
        P("rows"),
        P("rows"),
        P("rows"),
        P("rows", None, None),
        P(),
        P("cols", "rows"),
    )
    out_specs = (P("cols", "rows"), P("cols", "rows"), P(None, "cols"))
    return jax.shard_map(shards, mesh=mesh, in_specs=in_specs, out_specs=out_specs, check_vma=False)
```

```python
import functools

import jax
import jax.numpy as jnp
from jax import lax
from jax.experimental import pallas as pl
from jax.experimental.pallas import tpu as pltpu
from jax.sharding import PartitionSpec as P

BF16 = jnp.bfloat16
F32 = jnp.float32
I32 = jnp.int32
SLOTS = 8
STEP = 16
WAYS = 4
LONG = 8
PIECES = 8
VMEM = pl.BlockSpec(memory_space=pltpu.VMEM)
HBM = pl.BlockSpec(memory_space=pltpu.HBM)
SMEM = pl.BlockSpec(memory_space=pltpu.SMEM)
NN = (((1,), (0,)), ((), ()))
NT = (((1,), (1,)), ((), ()))
TN = (((0,), (0,)), ((), ()))


def params(**kw):
    return pltpu.CompilerParams(vmem_limit_bytes=20 << 20, **kw)


def cost(flops, bytes_accessed):
    return pl.CostEstimate(flops=flops, bytes_accessed=bytes_accessed, transcendentals=0)


def send_out(buf, out_hbm, sems, piece):
    size = buf.shape[0] // sems.shape[0]
    at = pl.ds(piece * size, size)
    return pltpu.make_async_copy(buf.at[at], out_hbm.at[at], sems.at[piece])


def over_cols(value, here):
    groups = value.shape[0]
    rings = groups // 2
    value = value.reshape(rings, 2, *value.shape[1:])
    core, ring = here % 2, here // 2
    kept = lax.dynamic_index_in_dim(value, core, 1, keepdims=False)
    passed = lax.dynamic_index_in_dim(value, 1 - core, 1, keepdims=False)
    passed = lax.ppermute(passed, "cols", [(i, i ^ 1) for i in range(groups)])
    both = jnp.stack([kept, passed], axis=1)
    parts = []
    for far in range(rings):
        part = lax.dynamic_index_in_dim(both, (ring + far) % rings, 0, keepdims=False)
        if far:
            pairs = [(i, (i + 2 * far) % groups) for i in range(groups)]
            part = lax.ppermute(part, "cols", pairs)
        parts.append(part)
    return jnp.stack(parts)


def along(value, steps, peers):
    if not steps:
        return value
    pairs = [(i, i // LONG * LONG + (i + steps) % LONG) for i in range(peers)]
    return lax.ppermute(value, "rows", pairs)


def in_hbm(x):
    return pltpu.with_memory_space_constraint(x, pltpu.HBM)


def dot(a, b, dims):
    return lax.dot_general(a, b, dims, preferred_element_type=F32)


def position(col):
    return ((col >> 8) * 2 + ((col >> 5) & 1)) * (LONG // 2) + ((col >> 6) & 3)


def ranks(col, peers):
    peer, block = position(col), col & 31
    of_peer = (lax.broadcasted_iota(I32, (peers, col.shape[1]), 0) == peer).astype(F32)
    of_block = (lax.broadcasted_iota(I32, (32, col.shape[1]), 0) == block).astype(F32)
    counts = dot(of_peer.astype(BF16), of_block.astype(BF16), NT)
    present = (counts > 0.5).astype(F32)
    before = lower(32).astype(F32)
    return of_peer, of_block, present, dot(present.astype(BF16), before.astype(BF16), NN)


def lower(n):
    return lax.broadcasted_iota(I32, (n, n), 0) < lax.broadcasted_iota(I32, (n, n), 1)


def start_kernel(
    row_hbm,
    col_hbm,
    features_hbm,
    order_hbm,
    want_hbm,
    out_ref,
    plan_ref,
    row_ref,
    col_ref,
    features_ref,
    order_ref,
    want_ref,
    blocked,
    sems,
):
    copies = [
        pltpu.make_async_copy(col_hbm, col_ref, sems.at[0]),
        pltpu.make_async_copy(features_hbm, features_ref, sems.at[1]),
        pltpu.make_async_copy(order_hbm, order_ref, sems.at[2]),
        pltpu.make_async_copy(row_hbm, row_ref, sems.at[4]),
    ]
    for copy in copies:
        copy.start()
    copies[0].wait()
    relays, turns, _ = want_ref.shape
    peers = relays * turns
    of_peer, of_block, present, rank = ranks(col_ref[...], peers)
    number = lax.broadcasted_iota(I32, (peers, 32), 1).astype(F32)
    lane = lax.broadcasted_iota(I32, (peers, 128), 1)
    want = jnp.zeros((peers, 128), F32)
    for s in range(SLOTS):
        chosen = jnp.sum(
            jnp.where(rank == float(s), present * number, 0.0), axis=1, keepdims=True
        )
        want = jnp.where(lane == s, chosen, want)
    want = want.astype(I32)
    for m in range(relays):
        want_ref[m] = want[m * turns : (m + 1) * turns, :]
    store = pltpu.make_async_copy(want_ref, want_hbm, sems.at[3])
    store.start()
    for copy in copies[1:]:
        copy.wait()
    plan_ref[...] = lay_out(peers, row_ref[...], col_ref[...], of_peer, of_block, rank)
    permute(features_ref, order_ref, out_ref, blocked)
    store.wait()


def lay_out(peers, row, col, of_peer, of_block, rank):
    tiles = col.shape[1]
    rank_of = dot(rank.astype(BF16), of_peer.astype(BF16), TN)
    tile_rank = jnp.sum(rank_of * of_block, axis=0, keepdims=True)
    own = ((col >> 5) == (row >> 5)).astype(F32)
    own_count = jnp.sum(own, axis=1, keepdims=True)
    earlier = lower(tiles).astype(F32).astype(BF16)
    far_peer = of_peer * (1.0 - own)
    same = dot(far_peer.astype(BF16), earlier, NN)
    totals = jnp.sum(far_peer, axis=1, keepdims=True)
    upper = (
        lax.broadcasted_iota(I32, (peers, peers), 0) > lax.broadcasted_iota(I32, (peers, peers), 1)
    ).astype(F32)
    wide = jnp.broadcast_to(totals, (peers, tiles))
    starts = dot(upper.astype(BF16), wide.astype(BF16), NN)
    ahead = jnp.sum(far_peer * (same + starts), axis=0, keepdims=True)
    own_ahead = dot(jnp.broadcast_to(own, (8, tiles)).astype(BF16), earlier, NN)[0:1]
    spot = jnp.where(own > 0.5, own_ahead, own_count + ahead)
    moved = (lax.broadcasted_iota(I32, (tiles, tiles), 0).astype(F32) == spot).astype(F32)
    values = jnp.concatenate(
        [
            lax.broadcasted_iota(I32, (1, tiles), 1).astype(F32),
            jnp.where(own > 0.5, float(peers), position(col).astype(F32)),
            jnp.where(own > 0.5, (col & 31).astype(F32), tile_rank),
            (row & 31).astype(F32),
            jnp.zeros((4, tiles), F32),
        ],
        axis=0,
    )
    ordered = dot(values.astype(BF16), moved.astype(BF16), NT)
    lanes = lax.broadcasted_iota(I32, (peers, tiles), 1)
    diagonal = (lanes == lax.broadcasted_iota(I32, (peers, tiles), 0)).astype(F32)
    firsts = own_count + jnp.sum(starts * diagonal, axis=0, keepdims=True)
    plan = jnp.concatenate(
        [
            ordered[0:1],
            ordered[1:2] * float(SLOTS) + ordered[2:3],
            ordered[3:4],
            jnp.broadcast_to(own_count, (1, tiles)),
            firsts,
            jnp.zeros((3, tiles), F32),
        ],
        axis=0,
    )
    return plan.astype(I32)


def pick_lanes(blocked, pick, high):
    width = 16
    spread = dot(blocked, pick, NN)
    total = jnp.zeros((width, pick.shape[1]), F32)
    for s in range(blocked.shape[0] // width):
        total = total + jnp.where(high == s, spread[s * width : (s + 1) * width], 0.0)
    return total.astype(BF16)


def permute(features_ref, order_ref, out_ref, blocked):
    count = order_ref.shape[0]
    width = features_ref.shape[0]
    for s in range(count):
        blocked[s * width : (s + 1) * width, :] = features_ref[:, s * 128 : (s + 1) * 128]
    low = lax.broadcasted_iota(I32, (128, 256), 0)
    for j in range(0, count, 2):
        o = jnp.concatenate([order_ref[j : j + 1, :], order_ref[j + 1 : j + 2, :]], axis=1)
        o = o & (count * 128 - 1)
        pick = jnp.where(low == (o & 127), 1.0, 0.0).astype(BF16)
        total = pick_lanes(blocked[...], pick, o >> 7)
        out_ref[j] = total[:, :128]
        out_ref[j + 1] = total[:, 128:]


def pack_kernel(here_ref, asked_ref, *refs):
    held, (send_hbm, buf, sems) = refs[:-3], refs[-3:]
    pieces = sems.shape[0]
    members = buf.shape[0] // pieces
    for piece in range(pieces):
        for m in range(piece * members, (piece + 1) * members):
            for far, blocks_ref in enumerate(held):
                k = (here_ref[0] + far) % len(held)
                for s in range(SLOTS):
                    buf[m, k * SLOTS + s] = blocks_ref[asked_ref[m, k, s]]
        send_out(buf, send_hbm, sems, piece).start()
    for piece in range(pieces):
        send_out(buf, send_hbm, sems, piece).wait()


def chunk_copy(tiles_hbm, tiles, sems, i):
    at = pl.ds(i * STEP, STEP)
    return pltpu.make_async_copy(tiles_hbm.at[at], tiles.at[at], sems.at[i])


def fetch_tiles(first, last, tiles_hbm, tiles, sems):
    def start(i, carry):
        chunk_copy(tiles_hbm, tiles, sems, i).start()
        return carry

    lax.fori_loop(first, last, start, 0)


def add_products(plan_ref, first, last, left, tile, dims, into, spare, prod, total, arrive=None):
    def step(i, carry):
        if arrive is not None:
            arrive(i)
        for u in range(STEP):
            k = i * STEP + u
            prod[u] = dot(left(k), tile(k), dims)
        for u in range(STEP):
            k = i * STEP + u
            at = jnp.where((k >= first) & (k < last), into(k), spare)
            total[at] = total[at] + prod[u]
        return carry

    lax.fori_loop(first // STEP, (last + STEP - 1) // STEP, step, 0)


def forward_own_kernel(base, plan_ref, own_ref, tiles_hbm, out_ref, list_hbm, prod, total, tiles, sem, out_sem):
    count = own_ref.shape[0]
    for k in range(tiles.shape[0]):
        pltpu.make_async_copy(tiles_hbm.at[plan_ref[0, k]], tiles.at[k], sem).start()
    pltpu.make_async_copy(tiles_hbm, tiles, sem).wait()
    store = pltpu.make_async_copy(tiles, list_hbm, out_sem)
    store.start()
    total[...] = jnp.zeros_like(total)
    add_products(
        plan_ref,
        0,
        plan_ref[3, 0],
        lambda k: own_ref[jnp.maximum(plan_ref[1, k] - base, 0)],
        lambda k: tiles[k],
        NT,
        lambda k: plan_ref[2, k],
        count,
        prod,
        total,
    )
    out_ref[...] = total[:count]
    store.wait()


def forward_kernel(plan_ref, got_ref, part_ref, tiles_hbm, out_ref, prod, total, tiles, sems):
    first = plan_ref[3, 0]

    fetch_tiles(first // STEP, tiles.shape[0] // STEP, tiles_hbm, tiles, sems)
    groups, per = out_ref.shape[:2]
    count = part_ref.shape[0]
    slots = got_ref.shape[0]
    total[:count] = part_ref[...]
    add_products(
        plan_ref,
        first,
        tiles.shape[0],
        lambda k: got_ref[jnp.minimum(plan_ref[1, k], slots - 1)],
        lambda k: tiles[k],
        NT,
        lambda k: plan_ref[2, k],
        count,
        prod,
        total,
        lambda i: chunk_copy(tiles_hbm, tiles, sems, i).wait(),
    )
    for c in range(groups):
        for b in range(per):
            out_ref[c, b] = total[c * per + b].astype(BF16)


def source(here, far, core):
    rings = 4
    y, c = here // 2, here % 2
    return (y + rings - far) % rings * 2 + (c + core) % 2


def dense_kernel(here_ref, weight_ref, got_ref, grad_ref, out_ref, act_hbm, grads, act_ref, sems):
    groups, per, width, _ = got_ref.shape
    for far in range(groups // 2):
        for core in range(2):
            grads[source(here_ref[0], far, core)] = grad_ref[far, core]
    inputs = groups * width
    weight = weight_ref[...]
    weight_t = weight.astype(F32).T.astype(BF16)
    part = jnp.zeros((inputs, inputs), F32)
    stores, pre_grads = [], []
    for b in range(per):
        agg = got_ref[:, b].reshape(inputs, 128)
        grad = grads[:, b].reshape(inputs, 128).astype(F32)
        pre = dot(weight_t, agg, NN)
        logistic = jax.nn.sigmoid(pre)
        act = (pre * logistic).astype(BF16)
        pre_grad = (grad * logistic * (1.0 + pre * (1.0 - logistic))).astype(BF16)
        pre_grads.append(pre_grad)
        act_ref[:, b] = act.reshape(groups, width, 128)
        store = pltpu.make_async_copy(act_ref.at[:, b], act_hbm.at[:, b], sems.at[b])
        store.start()
        stores.append(store)
    for b, pre_grad in enumerate(pre_grads):
        agg_grad = dot(weight, pre_grad, NN).astype(BF16)
        part = part + dot(pre_grad, got_ref[:, b].reshape(inputs, 128), NT)
        out_ref[:, b] = agg_grad.reshape(groups, width, 128)
    high = part.astype(BF16)
    out_ref[:, per] = high.reshape(groups, width, 128)
    out_ref[:, per + 1] = (part - high.astype(F32)).astype(BF16).reshape(groups, width, 128)
    for store in stores:
        store.wait()


def backward_kernel(plan_ref, got_ref, tiles, send_hbm, prod, total, buf, sems):
    last = tiles.shape[0] // STEP
    begin = jnp.minimum(plan_ref[3, 0] // STEP, last - 1)

    groups = got_ref.shape[0]
    per = got_ref.shape[1] - 2
    relays = buf.shape[0]
    each = buf.shape[1] - 1
    pieces = sems.shape[0]
    share = relays // pieces
    slots = relays * each
    total[...] = jnp.zeros_like(total)
    part = got_ref[0, per].astype(F32) + got_ref[0, per + 1].astype(F32)
    for c in range(1, groups):
        part = part + got_ref[c, per].astype(F32) + got_ref[c, per + 1].astype(F32)
    part = part.astype(BF16)
    for m in range(relays):
        buf[m, each] = part

    def step(i, carry):
        for u in range(STEP):
            r = plan_ref[2, i * STEP + u]
            prod[u] = dot(got_ref[r // per, r % per], tiles[i * STEP + u], NN)
        for u in range(STEP):
            k = i * STEP + u
            at = jnp.where(k >= plan_ref[3, 0], jnp.minimum(plan_ref[1, k], slots), slots)
            total[at] = total[at] + prod[u]
        done = (i + 1) * STEP
        for piece in range(pieces):
            until = plan_ref[4, (piece + 1) * share * each // SLOTS] if piece + 1 < pieces else last * STEP

            @pl.when((until <= done) & ((until > i * STEP) | (i == begin)))
            def _():
                for m in range(piece * share, (piece + 1) * share):
                    buf[m, :each] = total[m * each : (m + 1) * each].astype(BF16)
                send_out(buf, send_hbm, sems, piece).start()

        return carry

    lax.fori_loop(begin, last, step, 0)
    for piece in range(pieces):
        send_out(buf, send_hbm, sems, piece).wait()


def backward_own_kernel(
    base, plan_ref, got_ref, tiles_hbm, order_ref, out_hbm, inverse_ref, pick_ref, prod, total, tiles, sems, spots, low_pick, out_sem
):
    fetch_tiles(0, (plan_ref[3, 0] + STEP - 1) // STEP, tiles_hbm, tiles, sems)
    count, width = out_hbm.shape[:2]
    per = got_ref.shape[1] - 2
    total[...] = jnp.zeros_like(total)
    add_products(
        plan_ref,
        0,
        plan_ref[3, 0],
        lambda k: got_ref[plan_ref[2, k] // per, plan_ref[2, k] % per],
        lambda k: tiles[k],
        NN,
        lambda k: jnp.maximum(plan_ref[1, k] - base, 0),
        count,
        prod,
        total,
        lambda i: chunk_copy(tiles_hbm, tiles, sems, i).wait(),
    )
    store = pltpu.make_async_copy(total.at[pl.ds(0, count)], out_hbm, out_sem)
    store.start()
    low = lax.broadcasted_iota(I32, (128, 128), 0)
    source = lax.broadcasted_iota(I32, (count, 128), 0)
    lane = lax.broadcasted_iota(I32, (count, 128), 1).astype(F32)
    for j in range(count):
        o = order_ref[j : j + 1, :] & (count * 128 - 1)
        lanes = slice(j * 128, (j + 1) * 128)
        low_pick[:, lanes] = jnp.where(low == (o & 127), 1.0, 0.0).astype(BF16)
        here = source == (o >> 7)
        spots[:count, lanes] = jnp.where(here, float(j), 0.0).astype(BF16)
        spots[count:, lanes] = jnp.where(here, lane, 0.0).astype(BF16)
    inverse = dot(spots[...], low_pick[...], NT).astype(I32)
    odd = lax.broadcasted_iota(I32, (256, 128), 0)
    for j in range(count):
        at = inverse[count + j : count + j + 1, :] + (inverse[j : j + 1, :] & 1) * 128
        pick_ref[:, j * 128 : (j + 1) * 128] = jnp.where(odd == at, 1.0, 0.0).astype(BF16)
    inverse_ref[...] = inverse[:count] >> 1
    store.wait()


def blocks_kernel(grad_ref, out_ref):
    groups, per = out_ref.shape[:2]
    for c in range(groups):
        for b in range(per):
            at = (c * per + b) * 128
            out_ref[c, b] = grad_ref[:, at : at + 128]


def lanes_kernel(here_ref, got_ref, out_ref):
    for far in range(got_ref.shape[0]):
        for core in range(2):
            at = source(here_ref[0], far, core) * got_ref.shape[2]
            for b in range(got_ref.shape[2]):
                out_ref[:, pl.ds(pl.multiple_of((at + b) * 128, 128), 128)] = got_ref[far, core, b]


def relay_kernel(turn_ref, asked_ref, got_ref, own_ref, *refs):
    outs, totals = refs[: -WAYS], refs[-WAYS:]
    members, each = got_ref.shape[:2]
    each = each - 1
    turns = each // SLOTS
    count = own_ref.shape[0] - 1
    for total in totals:
        total[...] = jnp.zeros_like(total)
    for m in range(0, members, WAYS):
        for k in range(turns):
            for s in range(SLOTS):
                for w, total in enumerate(totals):
                    at = k * count + asked_ref[m + w, k, s]
                    total[at] = total[at] + got_ref[m + w, k * SLOTS + s].astype(F32)
    part = got_ref[0, each].astype(F32)
    for m in range(1, members):
        part = part + got_ref[m, each].astype(F32)
    own_ref[count] = part
    high = part.astype(BF16)
    low = (part - high.astype(F32)).astype(BF16)
    for far in range(turns):
        at = pl.ds((turn_ref[0] + far) % turns * count, count)
        value = totals[0][at]
        for total in totals[1:]:
            value = value + total[at]
        if far:
            outs[far - 1][:count] = value.astype(BF16)
            outs[far - 1][count] = high
            outs[far - 1][count + 1] = low
        else:
            own_ref[:count] = value


def final_kernel(scale, kept_hbm, own_ref, one_ref, two_ref, three_ref, inverse_ref, pick_ref, grads_ref, weight_ref, kept, sem):
    fetch = pltpu.make_async_copy(kept_hbm, kept, sem)
    fetch.start()
    count = kept.shape[0]
    part, node = own_ref[count], own_ref[:count]
    for ref in (one_ref, two_ref, three_ref):
        part = part + ref[count].astype(F32) + ref[count + 1].astype(F32)
        node = node + ref[:count].astype(F32)
    weight_ref[...] = part * scale
    fetch.wait()
    node = (node + kept[...]).astype(BF16)
    blocked = jnp.concatenate(
        [jnp.concatenate([node[j], node[j + 1]], axis=1) for j in range(0, count, 2)], axis=0
    )
    for j in range(0, count, 2):
        high = jnp.concatenate([inverse_ref[j : j + 1, :], inverse_ref[j + 1 : j + 2, :]], axis=1)
        lanes = slice(j * 128, (j + 2) * 128)
        grads_ref[:, lanes] = pick_lanes(blocked, pick_ref[:, lanes], high)


def shards(features, node_order, tile_row, tile_col, tile_vals, weight, grad_out):
    width, span = features.shape
    tiles, size, _ = tile_vals.shape
    count = span // size
    peers = lax.axis_size("rows")
    groups = lax.axis_size("cols")
    per = count // groups
    order = node_order.reshape(count, size)
    shape = jax.ShapeDtypeStruct
    prod = pltpu.VMEM((STEP, width, size), F32)
    tile_buf = pltpu.VMEM(tile_vals.shape, BF16)
    sums = lambda n: pltpu.VMEM((n + 1, width, size), F32)

    relays, turns = 2 * (peers // LONG), LONG // 2
    turn = lax.axis_index("rows") % LONG // 2
    turn_at = turn.reshape(1)
    near = [
        [x * LONG + 2 * j + q for x in range(peers // LONG) for q in range(2)] for j in range(turns)
    ]
    swap = lambda v: lax.all_to_all(v, "rows", 0, 0, tiled=True, axis_index_groups=near)

    with jax.named_scope("start"):
        rows, cols = tile_row.reshape(1, tiles), tile_col.reshape(1, tiles)
        want, own, plan = pl.pallas_call(
            start_kernel,
            out_shape=(
                pltpu.HBM((relays, turns, 128), I32),
                shape((count, width, size), BF16),
                shape((8, tiles), I32),
            ),
            in_specs=[HBM] * 4,
            out_specs=(HBM, VMEM, VMEM),
            scratch_shapes=[
                pltpu.VMEM((1, tiles), I32),
                pltpu.VMEM((1, tiles), I32),
                pltpu.VMEM((width, span), BF16),
                pltpu.VMEM((count, size), I32),
                pltpu.VMEM((relays, turns, 128), I32),
                pltpu.VMEM((count * width, size), BF16),
                pltpu.SemaphoreType.DMA((5,)),
            ],
            compiler_params=params(),
        )(in_hbm(rows), in_hbm(cols), in_hbm(features), in_hbm(order))
        held = [own] + [along(own, -2 * far, peers) for far in (2, 1, 3)]
        held = [held[0], held[2], held[1], held[3]]
        asked = swap(want)

    with jax.named_scope("pack"):
        send = pl.pallas_call(
            pack_kernel,
            out_shape=shape((relays, turns * SLOTS, width, size), BF16),
            in_specs=[SMEM, SMEM] + [VMEM] * turns,
            out_specs=HBM,
            scratch_shapes=[
                pltpu.VMEM((relays, turns * SLOTS, width, size), BF16),
                pltpu.SemaphoreType.DMA((min(PIECES, relays),)),
            ],
            compiler_params=params(),
        )(turn_at, asked, *held)
    with jax.named_scope("grads"):
        here = lax.axis_index("cols")
        grad_out, send = lax.optimization_barrier((grad_out, send))
        got = swap(send)

    with jax.named_scope("forward_own"):
        part, tile_list = pl.pallas_call(
            functools.partial(forward_own_kernel, peers * SLOTS),
            out_shape=(shape((count, width, size), F32), pltpu.HBM(tile_vals.shape, BF16)),
            in_specs=[SMEM, VMEM, HBM],
            out_specs=(VMEM, HBM),
            scratch_shapes=[prod, sums(count), tile_buf, pltpu.SemaphoreType.DMA, pltpu.SemaphoreType.DMA],
            compiler_params=params(),
            cost_estimate=cost(1 << 31, 1 << 22),
        )(plan, own, in_hbm(tile_vals))

    with jax.named_scope("grads"):
        grads = pl.pallas_call(
            blocks_kernel,
            out_shape=shape((groups, per, width, size), BF16),
            in_specs=[VMEM],
            out_specs=VMEM,
            compiler_params=params(),
        )(grad_out)
        grads, part = lax.optimization_barrier((over_cols(grads, here), part))
        here_at = here.reshape(1)

    with jax.named_scope("forward"):
        mixed = pl.pallas_call(
            forward_kernel,
            out_shape=shape((groups, per, width, size), BF16),
            in_specs=[SMEM, VMEM, VMEM, HBM],
            out_specs=VMEM,
            scratch_shapes=[prod, sums(count), tile_buf, pltpu.SemaphoreType.DMA((tiles // STEP,))],
            compiler_params=params(),
            cost_estimate=cost(1 << 30, 1 << 22),
        )(plan, got.reshape(peers * SLOTS, width, size), part, in_hbm(tile_list))
        mixed = lax.all_to_all(mixed, "cols", 0, 0, tiled=True)

    with jax.named_scope("dense"):
        back, act = pl.pallas_call(
            dense_kernel,
            out_shape=(
                shape((groups, per + 2, width, size), BF16),
                pltpu.HBM((groups, per, width, size), BF16),
            ),
            in_specs=[SMEM, VMEM, VMEM, VMEM],
            out_specs=(VMEM, HBM),
            scratch_shapes=[pltpu.VMEM((groups, per, width, size), BF16)] * 2
            + [pltpu.SemaphoreType.DMA((per,))],
            compiler_params=params(),
        )(here_at, weight, mixed, grads)
        back = lax.all_to_all(back, "cols", 0, 0, tiled=True)

    with jax.named_scope("backward"):
        parts = pl.pallas_call(
            backward_kernel,
            out_shape=shape((relays, turns * SLOTS + 1, width, size), BF16),
            in_specs=[SMEM, VMEM, VMEM],
            out_specs=HBM,
            scratch_shapes=[
                prod,
                sums(peers * SLOTS),
                pltpu.VMEM((relays, turns * SLOTS + 1, width, size), BF16),
                pltpu.SemaphoreType.DMA((4,)),
            ],
            compiler_params=params(),
            cost_estimate=cost(1 << 30, 1 << 22),
        )(plan, back, tile_list)
        parts = swap(parts)

    with jax.named_scope("backward_own"):
        kept, inverse, pick = pl.pallas_call(
            functools.partial(backward_own_kernel, peers * SLOTS),
            out_shape=(
                pltpu.HBM((count, width, size), F32),
                shape((count, size), I32),
                shape((2 * size, span), BF16),
            ),
            in_specs=[SMEM, VMEM, HBM, VMEM],
            out_specs=(HBM, VMEM, VMEM),
            scratch_shapes=[
                prod,
                sums(count),
                tile_buf,
                pltpu.SemaphoreType.DMA((tiles // STEP,)),
                pltpu.VMEM((2 * count, span), BF16),
                pltpu.VMEM((size, span), BF16),
                pltpu.SemaphoreType.DMA,
            ],
            compiler_params=params(),
            cost_estimate=cost(1 << 31, 1 << 22),
        )(plan, back, in_hbm(tile_list), order)

    with jax.named_scope("activated"):
        act, kept = lax.optimization_barrier((act, kept))
        activated = pl.pallas_call(
            lanes_kernel,
            out_shape=shape((width, span), BF16),
            in_specs=[SMEM, VMEM],
            out_specs=VMEM,
            compiler_params=params(),
        )(here_at, over_cols(act, here))

    with jax.named_scope("relay"):
        sums_of = pl.pallas_call(
            relay_kernel,
            out_shape=(shape((count + 1, width, size), F32),)
            + (shape((count + 2, width, size), BF16),) * (turns - 1),
            in_specs=[SMEM, SMEM, VMEM],
            out_specs=(VMEM,) * turns,
            scratch_shapes=[pltpu.VMEM((turns * count, width, size), F32)] * WAYS,
            compiler_params=params(),
        )(turn_at, asked, parts)
        passed = {far: along(sums_of[far], 2 * far, peers) for far in (2, 1, 3)}
        sums_of = [sums_of[0]] + [passed[far] for far in (1, 2, 3)]

    with jax.named_scope("final"):
        feat_grads, weight_grad = pl.pallas_call(
            functools.partial(final_kernel, float(peers * span) ** -0.5),
            out_shape=(shape((width, span), BF16), shape((width, size), F32)),
            in_specs=[HBM] + [VMEM] * (turns + 2),
            out_specs=(VMEM, VMEM),
            scratch_shapes=[pltpu.VMEM((count, width, size), F32), pltpu.SemaphoreType.DMA],
            compiler_params=params(),
        )(in_hbm(kept), *sums_of, inverse, pick)
    return activated, feat_grads, weight_grad.T


def solution(mesh):
    in_specs = (
        P("cols", "rows"),
        P("rows"),
        P("rows"),
        P("rows"),
        P("rows", None, None),
        P(),
        P("cols", "rows"),
    )
    out_specs = (P("cols", "rows"), P("cols", "rows"), P(None, "cols"))
    return jax.shard_map(shards, mesh=mesh, in_specs=in_specs, out_specs=out_specs, check_vma=False)
```
